32 devices in a mesh: group: 4 (over y, x), shard: 8 (over z, core).
Axes of the slice: x: 2, y: 2, z: 4, core: 2. Of those that a mesh axis runs over, the one named last changes fastest.
Arguments:
- tokens: bfloat16 [2048, 2048], P(('group', 'shard')), may hold values from -7 to 7
- w_qk: bfloat16 [2048, 1024], P('shard'), may hold values from -0.09375 to 0.09375
- w_in: bfloat16 [128, 2048], replicated, may hold values from -0.5 to 0.5
- w_out: bfloat16 [2048, 128], replicated, may hold values from -0.125 to 0.125
- particles: bfloat16 [131072, 128], P(('group', 'shard')), may hold values from -6 to 6
- cotangent: bfloat16 [131072, 128], P(('group', 'shard')), may hold values from -6 to 6
- clusters: int32 [131072], P(('group', 'shard')), may hold values from 0 to 63
- owners: int32 [1024], P(('group', 'shard')), may hold values from 0 to 7, as said below
Outputs:
- particle_out: bfloat16 [131072, 128], P(('group', 'shard'))
- qk_grad: float32 [2048, 1024], P('shard')
The draws below stay inside these ranges and needn't reach their ends.
Inputs may be any that keep to these rules, and one draw needn't show every extreme that they name: `owners`: each device's blocks name one owner at most 8 times; in every group some owner is named exactly 8 times by the blocks of every device of the group.
All inputs are finite; a program needn't handle non-finite values.
Results may differ from the reference program's by a relative error of at most 0.028.
Values may be sent and summed in bfloat16 or wider, within the bound.
No kernel may reach another device: no remote copies, remote signals or barrier semaphores. Data moves between devices by JAX's collectives and lax.ppermute only.
A program may use at most 64 MiB of HBM per device.

```python
import math
import jax
import jax.numpy as jnp
import numpy as np
from jax import lax

D = 2048
HEADS = 8
PW = 128
BLOCK = 128
T_DEV = 64
NB = 32
P_DEV = 4096
PARTICLES = 131072
TOKENS = 2048
QK = 1024
N_GROUP = 4
N_SHARD = 8


def draw_tokens(key, part):
    key_base = jax.random.fold_in(key, 11)
    return jnp.clip(jax.random.normal(key_base, (TOKENS, D), jnp.float32), -6.0, 6.0).astype(jnp.bfloat16)


def draw_owners(key, part):
    capacity = 2 * NB // N_SHARD
    num_devices = N_GROUP * N_SHARD
    slot_count = N_SHARD * capacity
    key_busy = jax.random.fold_in(key, 21)
    key_noise = jax.random.fold_in(key, 22)
    key_shuffle = jax.random.fold_in(key, 23)
    busiest = jax.random.randint(key_busy, (N_GROUP,), 0, N_SHARD)
    busiest_dev = jnp.repeat(busiest, N_SHARD)
    slot_owner = jnp.arange(slot_count, dtype=jnp.int32) // capacity
    noise_bits = jax.random.randint(key_noise, (num_devices, slot_count), 0, 1 << 20)
    slot_score = jnp.where(slot_owner[None, :] == busiest_dev[:, None], 0, noise_bits + 1)
    slot_score = slot_score * slot_count + jnp.arange(slot_count, dtype=jnp.int32)[None, :]
    slot_order = jnp.argsort(slot_score, axis=1)
    chosen = jnp.take(slot_owner, slot_order[:, :NB])
    shuffle_score = jax.random.randint(key_shuffle, (num_devices, NB), 0, 1 << 20) * NB + jnp.arange(NB, dtype=jnp.int32)[None, :]
    shuffle = jnp.argsort(shuffle_score, axis=1)
    chosen = jnp.take_along_axis(chosen, shuffle, axis=1)
    return chosen.reshape(num_devices * NB).astype(jnp.int32)


def plant(result, stream_key, low, top_value):
    extent = result.shape
    place = [jax.random.randint(jax.random.fold_in(stream_key, axis), (), 0, extent[axis]) for axis in range(len(extent))]
    result = result.at[tuple(place)].set(low)
    longest = extent.index(max(extent))
    place[longest] = (place[longest] + 1) % extent[longest]
    return result.at[tuple(place)].set(top_value)


def block_levels(rng, shape, shards, low, high):
    factor_of, own = 1.0, jax.random.fold_in(rng, 6)
    for dim, blocks in shards:
        heights = jnp.exp(jax.random.uniform(jax.random.fold_in(own, dim), (blocks,), jnp.float32, low / len(shards), high / len(shards)))
        factor_of = factor_of * jnp.repeat(heights, shape[dim] // blocks).reshape([-1 if axis == dim else 1 for axis in range(len(shape))])
    return factor_of


def cumulative_ranks(count, slope):
    loads = [(1 << 20) // math.isqrt(standing ** slope) + 1 for standing in range(1, count + 1)]
    width = 1 + sum(loads) // (1 << 30)
    return np.cumsum(np.array([max(1, weight // width) for weight in loads]))


def ranked_ids(own_key, shape, number_of, skew):
    table = cumulative_ranks(number_of, skew)
    lot = jax.random.randint(jax.random.fold_in(own_key, 1), shape, 0, int(table[number_of - 1]))
    rank = jnp.searchsorted(jnp.asarray(table, jnp.int32), lot, side="right")
    return jax.random.permutation(jax.random.fold_in(own_key, 2), number_of)[rank].astype(jnp.int32)


def scatter_about(key, shape, deviation, bound, split=(), kind=jnp.bfloat16):
    drawn = jax.random.normal(key, shape, jnp.float32) * deviation
    if len(split) > 0:
        drawn = block_levels(key, shape, split, -0.22, 0.18) * drawn
    return jnp.clip(drawn, min=-bound, max=bound).astype(kind)


def setup_inputs(seed: int = 0) -> dict:
    key_list = jax.random.split(jax.random.key(seed), 9)
    return {
        "tokens": draw_tokens(jax.random.fold_in(key_list[8], 71), 0),
        "w_qk": scatter_about(key_list[1], (D, QK), (2 * D) ** -0.5, 0.09375, ((0, 8),)),
        "w_in": scatter_about(key_list[2], (PW, D), PW ** -0.5, 0.5),
        "w_out": scatter_about(key_list[3], (D, PW), D ** -0.5, 0.125),
        "particles": scatter_about(key_list[4], (PARTICLES, PW), 1.0, 6.0, ((0, 32),)),
        "cotangent": scatter_about(key_list[5], (PARTICLES, PW), 1.0, 6.0, ((0, 32),)),
        "clusters": plant(ranked_ids(key_list[6], (PARTICLES,), T_DEV, 2), jax.random.fold_in(key_list[6], 3), 0, T_DEV - 1).astype(jnp.int32),
        "owners": draw_owners(jax.random.fold_in(key_list[8], 71), 0),
    }


def token_pass(tokens, pooled, w_qk, w_in, w_out, pooled_grad):
    hidden_sum = tokens.astype(jnp.float32) + jnp.dot(pooled, w_in, preferred_element_type=jnp.float32)
    hidden = hidden_sum.astype(jnp.bfloat16)
    queries = jnp.dot(hidden, w_qk, preferred_element_type=jnp.float32).astype(jnp.bfloat16)
    num_rows = hidden.shape[0]
    head_cols = queries.shape[1]
    q_heads = queries.reshape(num_rows, HEADS, -1).astype(jnp.float32)
    score_scale = 1.0 / math.sqrt(q_heads.shape[2])
    scores = jnp.einsum('ihd,jhd->hij', q_heads, q_heads) * score_scale
    self_mask = jnp.eye(num_rows, dtype=bool)
    scores = jnp.where(self_mask[None], -1000000000.0, scores)
    row_max = lax.optimization_barrier(jnp.max(scores, axis=2, keepdims=True))
    weights_exp = jnp.exp(scores - row_max)
    attn_prob = weights_exp / lax.optimization_barrier(jnp.sum(weights_exp, axis=2, keepdims=True))
    prob_low = lax.optimization_barrier(attn_prob.astype(jnp.bfloat16)).astype(jnp.float32)
    hidden_wide = hidden.astype(jnp.float32)
    values = hidden_wide[:, :head_cols].reshape(num_rows, HEADS, -1)
    attended = jnp.einsum('hij,jhv->ihv', prob_low, values).reshape(num_rows, head_cols)
    output = jnp.concatenate([hidden_wide[:, :head_cols] + attended, hidden_wide[:, head_cols:]], axis=1).astype(jnp.bfloat16)
    unpooled = jnp.dot(output, w_out, preferred_element_type=jnp.float32).astype(jnp.bfloat16)
    out_grad = jnp.dot(pooled_grad, w_out.T, preferred_element_type=jnp.float32).astype(jnp.bfloat16)
    grad_heads = out_grad[:, :head_cols].reshape(num_rows, HEADS, -1).astype(jnp.float32)
    prob_grad = jnp.einsum('ihv,jhv->hij', grad_heads, values)
    score_grad = attn_prob * (prob_grad - lax.optimization_barrier(jnp.sum(prob_grad * attn_prob, axis=2, keepdims=True))) * score_scale
    score_low = lax.optimization_barrier(score_grad.astype(jnp.bfloat16)).astype(jnp.float32)
    q_grad = jnp.einsum('hij,jhd->ihd', score_low, q_heads) + jnp.einsum('hji,jhd->ihd', score_low, q_heads)
    q_grad = q_grad.reshape(num_rows, -1).astype(jnp.bfloat16)
    return (unpooled, hidden, q_grad)

def reference(tokens, w_qk, w_in, w_out, particles, cotangent, clusters, owners):
    block_owner = jnp.repeat(owners, BLOCK)
    device_ids = jnp.arange(PARTICLES, dtype=jnp.int32) // P_DEV
    group_ids = device_ids // N_SHARD
    token_ids = ((group_ids * N_SHARD + block_owner) * T_DEV + clusters).astype(jnp.int32)
    counts = jax.ops.segment_sum(jnp.ones((PARTICLES,), jnp.float32), token_ids, TOKENS)
    pooled_sum = jax.ops.segment_sum(particles.astype(jnp.float32), token_ids, TOKENS)
    pooled = (pooled_sum / jnp.maximum(counts, 1.0)[:, None]).astype(jnp.bfloat16)
    pooled_grad = jax.ops.segment_sum(cotangent.astype(jnp.float32), token_ids, TOKENS).astype(jnp.bfloat16)
    num_devices = N_GROUP * N_SHARD

    def device_step(carry, inputs):
        tok_rows, pool_rows, grad_rows = inputs
        unpooled, hidden, q_grad = token_pass(tok_rows, pool_rows, w_qk, w_in, w_out, grad_rows)
        term = jnp.dot(hidden.T, q_grad, preferred_element_type=jnp.float32)
        term = lax.optimization_barrier(term.astype(jnp.bfloat16)).astype(jnp.float32)
        return (carry + term, unpooled)
    start_sum = jnp.zeros((D, QK), jnp.float32)
    qk_grad, unpooled = lax.scan(device_step, start_sum, (tokens.reshape(num_devices, T_DEV, D), pooled.reshape(num_devices, T_DEV, PW), pooled_grad.reshape(num_devices, T_DEV, PW)))
    all_unpooled = unpooled.reshape(TOKENS, PW)
    gathered = jnp.take(all_unpooled, token_ids, axis=0).astype(jnp.float32)
    particle_out = (particles.astype(jnp.float32) + gathered).astype(jnp.bfloat16)
    return (particle_out, qk_grad)
```

```python
import functools
import math

import jax
import jax.numpy as jnp
from jax import lax
from jax.experimental import pallas as pl
from jax.experimental.pallas import tpu as pltpu
from jax.sharding import PartitionSpec as P

HEADS = 8
F32 = jnp.float32
BF16 = jnp.bfloat16
VMEM = pl.BlockSpec(memory_space=pltpu.VMEM)


def params(mib):
    return pltpu.CompilerParams(vmem_limit_bytes=mib << 20)


def contract(a, b, da, db):
    return lax.dot_general(a, b, (((da,), (db,)), ((), ())), preferred_element_type=F32)


def pool_kernel(t_rows, owners_ref, clusters_ref, feat_ref, grad_ref, keep_ref, give_ref, acc_ref):
    step = pl.program_id(0)
    blocks, rows = clusters_ref.shape
    width = feat_ref.shape[1]

    @pl.when(step == 0)
    def _():
        acc_ref[...] = jnp.zeros_like(acc_ref)

    token = lax.broadcasted_iota(jnp.int32, (t_rows, rows), 0)
    for b in range(blocks):
        member = (clusters_ref[b : b + 1, :] == token).astype(F32)
        span = pl.ds(b * rows, rows)
        both = jnp.concatenate([feat_ref[span, :], grad_ref[span, :]], axis=1)
        sums = jnp.dot(member.astype(BF16), both, preferred_element_type=F32)
        place = pl.ds(pl.multiple_of(owners_ref[step * blocks + b] * t_rows, t_rows), t_rows)
        acc_ref[place, : 2 * width] += sums
        acc_ref[place, 2 * width :] += member

    @pl.when(step == pl.num_programs(0) - 1)
    def _():
        me = lax.axis_index("shard")
        for k in range(keep_ref.shape[0]):
            mine = me ^ (2 * k)
            keep_ref[k] = acc_ref[pl.ds(pl.multiple_of(mine * t_rows, t_rows), t_rows), :]
            other = mine ^ 1
            give_ref[k] = acc_ref[
                pl.ds(pl.multiple_of(other * t_rows, t_rows), t_rows), :
            ].astype(BF16)


def pool(particles, cotangent, clusters, owners, t_rows, n_shard):
    num_blocks = owners.shape[0]
    count, width = particles.shape
    rows = count // num_blocks
    steps = 4
    shape = (n_shard // 2, t_rows, 2 * width + rows)
    whole = pl.BlockSpec(shape, lambda i, own: (0, 0, 0))
    return pl.pallas_call(
        functools.partial(pool_kernel, t_rows),
        grid_spec=pltpu.PrefetchScalarGridSpec(
            num_scalar_prefetch=1,
            grid=(steps,),
            in_specs=[
                pl.BlockSpec((num_blocks // steps, rows), lambda i, own: (i, 0)),
                pl.BlockSpec((count // steps, width), lambda i, own: (i, 0)),
                pl.BlockSpec((count // steps, width), lambda i, own: (i, 0)),
            ],
            out_specs=[whole, whole],
            scratch_shapes=[pltpu.VMEM((n_shard * t_rows, shape[2]), F32)],
        ),
        out_shape=[jax.ShapeDtypeStruct(shape, F32), jax.ShapeDtypeStruct(shape, BF16)],
        compiler_params=params(24),
        name="pool",
    )(owners, clusters.reshape(num_blocks, rows), particles, cotangent)


def attend_kernel(parts, *refs):
    tok = refs[:parts]
    pooled_refs = refs[parts : 2 * parts]
    near, far, w_in, w_out, up_ref, keep_ref, give_ref, weight, hid, term = refs[2 * parts :]
    pairs, rows, cols = near.shape
    t_rows, width = tok[0].shape
    head_cols = cols * parts
    channels = w_in.shape[0]
    group, me = lax.axis_index("group"), lax.axis_index("shard")
    part = lax.rem(group, parts)
    core = lax.rem(me, 2)
    pair = lax.div(me, 2)
    for k in range(pairs):
        base = (pair ^ k) * (2 * rows)
        weight[pl.ds(pl.multiple_of(base + core * rows, rows), rows), :] = near[k]
        weight[pl.ds(pl.multiple_of(base + (1 - core) * rows, rows), rows), :] = far[k]
    pooled = jnp.concatenate([r[:, :channels] for r in pooled_refs], axis=0)
    pooled_grad = jnp.concatenate([r[:, channels:] for r in pooled_refs], axis=0)
    step = 512
    for n in range(0, width, step):
        wide = jnp.dot(pooled, w_in[:, n : n + step], preferred_element_type=F32)
        for k in range(parts):
            span = slice(k * t_rows, (k + 1) * t_rows)
            hid[span, n : n + step] = (
                tok[k][:, n : n + step].astype(F32) + wide[span]
            ).astype(BF16)
    queries = jnp.dot(hid[...], weight[...], preferred_element_type=F32).astype(BF16)
    first = pl.ds(pl.multiple_of(part * cols, cols), cols)
    values = hid[:, first]
    out_w = w_out[first, :]
    out_grad = contract(pooled_grad, out_w, 1, 1).astype(BF16)
    dim = head_cols // HEADS
    scale = 1.0 / math.sqrt(dim)
    total = parts * t_rows
    row = lax.broadcasted_iota(jnp.int32, (total, total), 0)
    col = lax.broadcasted_iota(jnp.int32, (total, total), 1)
    same = lax.div(row, t_rows) == lax.div(col, t_rows)
    outs, grads = [], []
    for h in range(cols // dim):
        lanes = slice(h * dim, (h + 1) * dim)
        q, v, g = queries[:, lanes], values[:, lanes], out_grad[:, lanes]
        scores = contract(q, q, 1, 1) * scale
        scores = jnp.where(row == col, -1000000000.0, scores)
        scores = jnp.where(same, scores, -3.0e38)
        e = jnp.exp(scores - jnp.max(scores, axis=1, keepdims=True))
        prob = e / jnp.sum(e, axis=1, keepdims=True)
        attended = jnp.dot(prob.astype(BF16), v, preferred_element_type=F32)
        outs.append((v.astype(F32) + attended).astype(BF16))
        prob_grad = contract(g, v, 1, 1)
        inner = jnp.sum(prob_grad * prob, axis=1, keepdims=True)
        score_grad = (prob * (prob_grad - inner) * scale).astype(BF16)
        grads.append(
            jnp.dot(score_grad, q, preferred_element_type=F32) + contract(score_grad, q, 0, 0)
        )
    output = jnp.concatenate(outs, axis=1)
    q_grad = jnp.concatenate(grads, axis=1).astype(BF16)
    rest = (width - head_cols) // parts
    second = pl.ds(pl.multiple_of(head_cols + part * rest, rest), rest)
    up = jnp.dot(output, out_w, preferred_element_type=F32) + jnp.dot(
        hid[:, second], w_out[second, :], preferred_element_type=F32
    )
    for k in range(parts):
        up_ref[k] = up[k * t_rows : (k + 1) * t_rows].astype(BF16)
    for k in range(pairs):
        chunk = pl.ds(pl.multiple_of((pair ^ k) * (2 * rows), 2 * rows), 2 * rows)
        term[...] = contract(hid[:, chunk], q_grad, 0, 0)
        keep_ref[k] = term[pl.ds(pl.multiple_of(core * rows, rows), rows), :].astype(BF16)
        give_ref[k] = term[pl.ds(pl.multiple_of((1 - core) * rows, rows), rows), :].astype(BF16)


def attend(tok, pooled, near, far, w_in, w_out):
    parts = len(tok)
    t_rows, width = tok[0].shape
    pairs, rows, cols = near.shape
    channels = w_in.shape[0]
    shape = jax.ShapeDtypeStruct((pairs, rows, cols), BF16)
    return pl.pallas_call(
        functools.partial(attend_kernel, parts),
        in_specs=[VMEM] * (2 * parts + 4),
        out_specs=[VMEM] * 3,
        out_shape=[jax.ShapeDtypeStruct((parts, t_rows, channels), BF16), shape, shape],
        scratch_shapes=[
            pltpu.VMEM((width, cols), BF16),
            pltpu.VMEM((parts * t_rows, width), BF16),
            pltpu.VMEM((2 * rows, cols), F32),
        ],
        compiler_params=params(24),
        name="attend",
    )(*tok, *pooled, near, far, w_in, w_out)


def unpool_kernel(owners_ref, clusters_ref, feat_ref, near, far, out_ref, rows_ref):
    step = pl.program_id(0)
    blocks, rows = clusters_ref.shape
    pairs, t_rows, _ = near.shape

    @pl.when(step == 0)
    def _():
        me = lax.axis_index("shard")
        for k in range(pairs):
            mine = me ^ (2 * k)
            rows_ref[pl.ds(pl.multiple_of(mine * t_rows, t_rows), t_rows), :] = near[k]
            rows_ref[pl.ds(pl.multiple_of((mine ^ 1) * t_rows, t_rows), t_rows), :] = far[k]

    token = lax.broadcasted_iota(jnp.int32, (t_rows, rows), 0)
    for b in range(blocks):
        member = (clusters_ref[b : b + 1, :] == token).astype(F32).astype(BF16)
        place = pl.ds(pl.multiple_of(owners_ref[step * blocks + b] * t_rows, t_rows), t_rows)
        span = pl.ds(b * rows, rows)
        picked = contract(member, rows_ref[place, :], 0, 0)
        out_ref[span, :] = (feat_ref[span, :].astype(F32) + picked).astype(BF16)


def unpool(particles, clusters, owners, near, far):
    num_blocks = owners.shape[0]
    count, width = particles.shape
    rows = count // num_blocks
    steps = 4
    pairs, t_rows, _ = near.shape
    whole = pl.BlockSpec(near.shape, lambda i, own: (0, 0, 0))
    return pl.pallas_call(
        unpool_kernel,
        grid_spec=pltpu.PrefetchScalarGridSpec(
            num_scalar_prefetch=1,
            grid=(steps,),
            in_specs=[
                pl.BlockSpec((num_blocks // steps, rows), lambda i, own: (i, 0)),
                pl.BlockSpec((count // steps, width), lambda i, own: (i, 0)),
                whole,
                whole,
            ],
            out_specs=pl.BlockSpec((count // steps, width), lambda i, own: (i, 0)),
            scratch_shapes=[pltpu.VMEM((2 * pairs * t_rows, width), BF16)],
        ),
        out_shape=jax.ShapeDtypeStruct(particles.shape, BF16),
        compiler_params=params(16),
        name="unpool",
    )(owners, clusters.reshape(num_blocks, rows), particles, near, far)


def spread_kernel(*refs):
    pieces, out_ref = refs[:-1], refs[-1]
    part = lax.rem(lax.axis_index("group"), len(pieces))
    cols = pieces[0].shape[1]
    for k, piece in enumerate(pieces):
        out_ref[:, pl.ds(pl.multiple_of((part ^ k) * cols, cols), cols)] = piece[...].astype(F32)


def spread(pieces):
    rows, cols = pieces[0].shape
    return pl.pallas_call(
        spread_kernel,
        in_specs=[VMEM] * len(pieces),
        out_specs=VMEM,
        out_shape=jax.ShapeDtypeStruct((rows, cols * len(pieces)), F32),
        compiler_params=params(16),
        name="spread",
    )(*pieces)


def swap(x, axis, k):
    n = lax.axis_size(axis)
    return lax.ppermute(x, axis, [(i, i ^ k) for i in range(n)])


def local(tokens, w_qk, w_in, w_out, particles, cotangent, clusters, owners):
    n_group, n_shard = lax.axis_size("group"), lax.axis_size("shard")
    parts = math.gcd(n_group, 4)
    pairs = n_shard // 2
    t_rows = tokens.shape[0]
    cols = w_qk.shape[1] // parts
    part = lax.rem(lax.axis_index("group"), parts)

    w_own = lax.dynamic_slice_in_dim(w_qk, part * cols, cols, axis=1)
    near = [w_own] + [swap(w_own, "shard", 2 * k) for k in range(1, pairs)]
    tok = [tokens] + [swap(tokens, "group", k) for k in range(1, parts)]
    near = jnp.stack(near)
    far = swap(near, "shard", 1)

    keep, give = pool(particles, cotangent, clusters, owners, t_rows, n_shard)
    joined = keep + swap(give, "shard", 1).astype(F32)
    sums = joined[0]
    for k in range(1, pairs):
        sums = sums + swap(joined[k].astype(BF16), "shard", 2 * k).astype(F32)
    channels = particles.shape[1]
    counts = jnp.sum(sums[:, 2 * channels :], axis=1, keepdims=True)
    pooled = jnp.concatenate(
        [sums[:, :channels] / jnp.maximum(counts, 1.0), sums[:, channels : 2 * channels]], axis=1
    ).astype(BF16)
    pooled = [pooled] + [swap(pooled, "group", k) for k in range(1, parts)]

    up, keep, give = attend(tok, pooled, near, far, w_in, w_out)

    joined = keep.astype(F32) + swap(give, "shard", 1).astype(F32)
    unpooled = up[0].astype(F32)
    for k in range(1, parts):
        unpooled = unpooled + swap(up[k], "group", k).astype(F32)
    unpooled = unpooled.astype(BF16)
    near = jnp.stack([unpooled] + [swap(unpooled, "shard", 2 * k) for k in range(1, pairs)])
    far = swap(near, "shard", 1)
    particle_out = unpool(particles, clusters, owners, near, far)

    grad = joined[0]
    for k in range(1, pairs):
        grad = grad + swap(joined[k].astype(BF16), "shard", 2 * k).astype(F32)
    if n_group > parts:
        part_sum = grad.astype(BF16)
        for k in range(1, n_group // parts):
            grad = grad + swap(part_sum, "group", k * parts).astype(F32)
    grad = grad.astype(BF16)
    qk_grad = spread([grad] + [swap(grad, "group", k) for k in range(1, parts)])
    return (particle_out, qk_grad)


def solution(mesh):
    placed = (
        P(("group", "shard"), None),
        P("shard", None),
        P(),
        P(),
        P(("group", "shard"), None),
        P(("group", "shard"), None),
        P(("group", "shard")),
        P(("group", "shard")),
    )
    return jax.shard_map(
        local,
        mesh=mesh,
        in_specs=placed,
        out_specs=(P(("group", "shard"), None), P("shard", None)),
        check_vma=False,
    )
```

```python
import functools
import math

import jax
import jax.numpy as jnp
from jax import lax
from jax.experimental import pallas as pl
from jax.experimental.pallas import tpu as pltpu
from jax.sharding import PartitionSpec as P

HEADS = 8
F32 = jnp.float32
BF16 = jnp.bfloat16
VMEM = pl.BlockSpec(memory_space=pltpu.VMEM)


def params(mib):
    return pltpu.CompilerParams(vmem_limit_bytes=mib << 20)


def contract(a, b, da, db):
    return lax.dot_general(a, b, (((da,), (db,)), ((), ())), preferred_element_type=F32)


def pool_kernel(t_rows, owners_ref, clusters_ref, feat_ref, grad_ref, keep_ref, give_ref, acc_ref):
    step = pl.program_id(0)
    blocks, rows = clusters_ref.shape
    width = feat_ref.shape[1]

    @pl.when(step == 0)
    def _():
        acc_ref[...] = jnp.zeros_like(acc_ref)

    token = lax.broadcasted_iota(jnp.int32, (t_rows, rows), 0)
    for b in range(blocks):
        member = (clusters_ref[b : b + 1, :] == token).astype(F32)
        span = pl.ds(b * rows, rows)
        both = jnp.concatenate([feat_ref[span, :], grad_ref[span, :]], axis=1)
        sums = jnp.dot(member.astype(BF16), both, preferred_element_type=F32)
        place = pl.ds(pl.multiple_of(owners_ref[step * blocks + b] * t_rows, t_rows), t_rows)
        acc_ref[place, : 2 * width] += sums
        acc_ref[place, 2 * width :] += member

    @pl.when(step == pl.num_programs(0) - 1)
    def _():
        me = lax.axis_index("shard")
        for k in range(keep_ref.shape[0]):
            mine = me ^ other_chip(k)
            keep_ref[k] = acc_ref[pl.ds(pl.multiple_of(mine * t_rows, t_rows), t_rows), :]
            other = mine ^ 1
            give_ref[k] = acc_ref[
                pl.ds(pl.multiple_of(other * t_rows, t_rows), t_rows), :
            ].astype(BF16)


def pool(particles, cotangent, clusters, owners, t_rows, n_shard):
    num_blocks = owners.shape[0]
    count, width = particles.shape
    rows = count // num_blocks
    steps = 4
    shape = (n_shard // 2, t_rows, 2 * width + rows)
    whole = pl.BlockSpec(shape, lambda i, own: (0, 0, 0))
    return pl.pallas_call(
        functools.partial(pool_kernel, t_rows),
        grid_spec=pltpu.PrefetchScalarGridSpec(
            num_scalar_prefetch=1,
            grid=(steps,),
            in_specs=[
                pl.BlockSpec((num_blocks // steps, rows), lambda i, own: (i, 0)),
                pl.BlockSpec((count // steps, width), lambda i, own: (i, 0)),
                pl.BlockSpec((count // steps, width), lambda i, own: (i, 0)),
            ],
            out_specs=[whole, whole],
            scratch_shapes=[pltpu.VMEM((n_shard * t_rows, shape[2]), F32)],
        ),
        out_shape=[jax.ShapeDtypeStruct(shape, F32), jax.ShapeDtypeStruct(shape, BF16)],
        compiler_params=params(24),
        name="pool",
    )(owners, clusters.reshape(num_blocks, rows), particles, cotangent)


def attend_kernel(parts, *refs):
    tok = refs[:parts]
    pooled_refs = refs[parts : 2 * parts]
    near, far, w_in, w_out, up_ref, keep_ref, give_ref, weight, hid, term = refs[2 * parts :]
    pairs, rows, cols = near.shape
    t_rows, width = tok[0].shape
    head_cols = cols * parts
    channels = w_in.shape[0]
    group, me = lax.axis_index("group"), lax.axis_index("shard")
    part = lax.rem(group, parts)
    core = lax.rem(me, 2)
    pair = lax.div(me, 2)
    for k in range(pairs):
        mine = me ^ other_chip(k)
        weight[pl.ds(pl.multiple_of(mine * rows, rows), rows), :] = near[k]
        weight[pl.ds(pl.multiple_of((mine ^ 1) * rows, rows), rows), :] = far[k]
    pooled = jnp.concatenate([r[:, :channels] for r in pooled_refs], axis=0)
    pooled_grad = jnp.concatenate([r[:, channels:] for r in pooled_refs], axis=0)
    step = 512
    for n in range(0, width, step):
        wide = jnp.dot(pooled, w_in[:, n : n + step], preferred_element_type=F32)
        for k in range(parts):
            span = slice(k * t_rows, (k + 1) * t_rows)
            hid[span, n : n + step] = (
                tok[k][:, n : n + step].astype(F32) + wide[span]
            ).astype(BF16)
    queries = jnp.dot(hid[...], weight[...], preferred_element_type=F32).astype(BF16)
    first = pl.ds(pl.multiple_of(part * cols, cols), cols)
    values = hid[:, first]
    out_w = w_out[first, :]
    out_grad = contract(pooled_grad, out_w, 1, 1).astype(BF16)
    dim = head_cols // HEADS
    scale = 1.0 / math.sqrt(dim)
    total = parts * t_rows
    row = lax.broadcasted_iota(jnp.int32, (total, total), 0)
    col = lax.broadcasted_iota(jnp.int32, (total, total), 1)
    same = lax.div(row, t_rows) == lax.div(col, t_rows)
    outs, grads = [], []
    for h in range(cols // dim):
        lanes = slice(h * dim, (h + 1) * dim)
        q, v, g = queries[:, lanes], values[:, lanes], out_grad[:, lanes]
        scores = contract(q, q, 1, 1) * scale
        scores = jnp.where(row == col, -1000000000.0, scores)
        scores = jnp.where(same, scores, -3.0e38)
        e = jnp.exp(scores - jnp.max(scores, axis=1, keepdims=True))
        prob = e / jnp.sum(e, axis=1, keepdims=True)
        attended = jnp.dot(prob.astype(BF16), v, preferred_element_type=F32)
        outs.append((v.astype(F32) + attended).astype(BF16))
        prob_grad = contract(g, v, 1, 1)
        inner = jnp.sum(prob_grad * prob, axis=1, keepdims=True)
        score_grad = (prob * (prob_grad - inner) * scale).astype(BF16)
        grads.append(
            jnp.dot(score_grad, q, preferred_element_type=F32) + contract(score_grad, q, 0, 0)
        )
    output = jnp.concatenate(outs, axis=1)
    q_grad = jnp.concatenate(grads, axis=1).astype(BF16)
    rest = (width - head_cols) // parts
    second = pl.ds(pl.multiple_of(head_cols + part * rest, rest), rest)
    up = jnp.dot(output, out_w, preferred_element_type=F32) + jnp.dot(
        hid[:, second], w_out[second, :], preferred_element_type=F32
    )
    for k in range(parts):
        up_ref[k] = up[k * t_rows : (k + 1) * t_rows].astype(BF16)
    for k in range(pairs):
        chunk = pl.ds(pl.multiple_of((pair ^ k) * (2 * rows), 2 * rows), 2 * rows)
        term[...] = contract(hid[:, chunk], q_grad, 0, 0)
        mine = core ^ 1 if k else core
        keep_ref[k] = term[pl.ds(pl.multiple_of(mine * rows, rows), rows), :].astype(BF16)
        give_ref[k] = term[pl.ds(pl.multiple_of((1 - mine) * rows, rows), rows), :].astype(BF16)


def attend(tok, pooled, near, far, w_in, w_out):
    parts = len(tok)
    t_rows, width = tok[0].shape
    pairs, rows, cols = near.shape
    channels = w_in.shape[0]
    shape = jax.ShapeDtypeStruct((pairs, rows, cols), BF16)
    return pl.pallas_call(
        functools.partial(attend_kernel, parts),
        in_specs=[VMEM] * (2 * parts + 4),
        out_specs=[VMEM] * 3,
        out_shape=[jax.ShapeDtypeStruct((parts, t_rows, channels), BF16), shape, shape],
        scratch_shapes=[
            pltpu.VMEM((width, cols), BF16),
            pltpu.VMEM((parts * t_rows, width), BF16),
            pltpu.VMEM((2 * rows, cols), F32),
        ],
        compiler_params=params(24),
        name="attend",
    )(*tok, *pooled, near, far, w_in, w_out)


def unpool_kernel(owners_ref, clusters_ref, feat_ref, near, far, out_ref, rows_ref):
    step = pl.program_id(0)
    blocks, rows = clusters_ref.shape
    pairs, t_rows, _ = near.shape

    @pl.when(step == 0)
    def _():
        me = lax.axis_index("shard")
        for k in range(pairs):
            mine = me ^ other_chip(k)
            rows_ref[pl.ds(pl.multiple_of(mine * t_rows, t_rows), t_rows), :] = near[k]
            rows_ref[pl.ds(pl.multiple_of((mine ^ 1) * t_rows, t_rows), t_rows), :] = far[k]

    token = lax.broadcasted_iota(jnp.int32, (t_rows, rows), 0)
    for b in range(blocks):
        member = (clusters_ref[b : b + 1, :] == token).astype(F32).astype(BF16)
        place = pl.ds(pl.multiple_of(owners_ref[step * blocks + b] * t_rows, t_rows), t_rows)
        span = pl.ds(b * rows, rows)
        picked = contract(member, rows_ref[place, :], 0, 0)
        out_ref[span, :] = (feat_ref[span, :].astype(F32) + picked).astype(BF16)


def unpool(particles, clusters, owners, near, far):
    num_blocks = owners.shape[0]
    count, width = particles.shape
    rows = count // num_blocks
    steps = 4
    pairs, t_rows, _ = near.shape
    whole = pl.BlockSpec(near.shape, lambda i, own: (0, 0, 0))
    return pl.pallas_call(
        unpool_kernel,
        grid_spec=pltpu.PrefetchScalarGridSpec(
            num_scalar_prefetch=1,
            grid=(steps,),
            in_specs=[
                pl.BlockSpec((num_blocks // steps, rows), lambda i, own: (i, 0)),
                pl.BlockSpec((count // steps, width), lambda i, own: (i, 0)),
                whole,
                whole,
            ],
            out_specs=pl.BlockSpec((count // steps, width), lambda i, own: (i, 0)),
            scratch_shapes=[pltpu.VMEM((2 * pairs * t_rows, width), BF16)],
        ),
        out_shape=jax.ShapeDtypeStruct(particles.shape, BF16),
        compiler_params=params(16),
        name="unpool",
    )(owners, clusters.reshape(num_blocks, rows), particles, near, far)


def spread_kernel(*refs):
    pieces, out_ref = refs[:-1], refs[-1]
    part = lax.rem(lax.axis_index("group"), len(pieces))
    cols = pieces[0].shape[1]
    for k, piece in enumerate(pieces):
        out_ref[:, pl.ds(pl.multiple_of((part ^ k) * cols, cols), cols)] = piece[...].astype(F32)


def spread(pieces):
    rows, cols = pieces[0].shape
    return pl.pallas_call(
        spread_kernel,
        in_specs=[VMEM] * len(pieces),
        out_specs=VMEM,
        out_shape=jax.ShapeDtypeStruct((rows, cols * len(pieces)), F32),
        compiler_params=params(16),
        name="spread",
    )(*pieces)


def swap(x, group, shard):
    n = lax.axis_size("shard")
    flip = group * n + shard
    pairs = [(i, i ^ flip) for i in range(lax.axis_size("group") * n)]
    return lax.ppermute(x, ("group", "shard"), pairs)


def other_chip(k):
    return 2 * k + 1 if k else 0


def local(tokens, w_qk, w_in, w_out, particles, cotangent, clusters, owners):
    n_group, n_shard = lax.axis_size("group"), lax.axis_size("shard")
    parts = math.gcd(n_group, 4)
    pairs = n_shard // 2
    t_rows = tokens.shape[0]
    cols = w_qk.shape[1] // parts
    part = lax.rem(lax.axis_index("group"), parts)

    w_own = lax.dynamic_slice_in_dim(w_qk, part * cols, cols, axis=1)
    near = [w_own] + [swap(w_own, 0, other_chip(k)) for k in range(1, pairs)]
    tok = [tokens] + [swap(tokens, k, 1) for k in range(1, parts)]
    owners, near[1] = lax.optimization_barrier((owners, near[1]))
    near = jnp.stack(near)
    far = swap(near, 0, 1)

    keep, give = pool(particles, cotangent, clusters, owners, t_rows, n_shard)
    joined = keep + swap(give, 0, 1).astype(F32)
    sums = joined[0]
    for k in range(1, pairs):
        sums = sums + swap(joined[k].astype(BF16), 0, other_chip(k)).astype(F32)
    channels = particles.shape[1]
    counts = jnp.sum(sums[:, 2 * channels :], axis=1, keepdims=True)
    pooled = jnp.concatenate(
        [sums[:, :channels] / jnp.maximum(counts, 1.0), sums[:, channels : 2 * channels]], axis=1
    ).astype(BF16)
    pooled = [pooled] + [swap(pooled, k, 1) for k in range(1, parts)]

    up, keep, give = attend(tok, pooled, near, far, w_in, w_out)

    joined = keep.astype(F32) + swap(give, 0, 1).astype(F32)
    up, joined = lax.optimization_barrier((up, joined))
    unpooled = up[0].astype(F32)
    for k in range(1, parts):
        unpooled = unpooled + swap(up[k], k, 1).astype(F32)
    unpooled = unpooled.astype(BF16)
    near = jnp.stack([unpooled] + [swap(unpooled, 0, other_chip(k)) for k in range(1, pairs)])
    far = swap(near, 0, 1)
    particle_out = unpool(particles, clusters, owners, near, far)

    grad = joined[0]
    for k in range(1, pairs):
        grad = grad + swap(joined[k].astype(BF16), 0, other_chip(k)).astype(F32)
    if n_group > parts:
        part_sum = grad.astype(BF16)
        for k in range(1, n_group // parts):
            grad = grad + swap(part_sum, k * parts, 0).astype(F32)
    grad = grad.astype(BF16)
    qk_grad = spread([grad] + [swap(grad, k, 0) for k in range(1, parts)])
    return (particle_out, qk_grad)


def solution(mesh):
    placed = (
        P(("group", "shard"), None),
        P("shard", None),
        P(),
        P(),
        P(("group", "shard"), None),
        P(("group", "shard"), None),
        P(("group", "shard")),
        P(("group", "shard")),
    )
    return jax.shard_map(
        local,
        mesh=mesh,
        in_specs=placed,
        out_specs=(P(("group", "shard"), None), P("shard", None)),
        check_vma=False,
    )
```

```python
import functools
import math

import jax
import jax.numpy as jnp
from jax import lax
from jax.experimental import pallas as pl
from jax.experimental.pallas import tpu as pltpu
from jax.sharding import PartitionSpec as P

HEADS = 8
F32 = jnp.float32
BF16 = jnp.bfloat16
VMEM = pl.BlockSpec(memory_space=pltpu.VMEM)


def params(mib):
    return pltpu.CompilerParams(vmem_limit_bytes=mib << 20)


def contract(a, b, da, db):
    return lax.dot_general(a, b, (((da,), (db,)), ((), ())), preferred_element_type=F32)


def pool_kernel(
    owners_hbm, clusters_hbm, feat_hbm, grad_hbm, keep_ref, give_ref, acc_ref, rows_ref, sems, owners_ref, clusters_ref
):
    blocks, rows = clusters_ref.shape
    pairs, t_rows, _ = keep_ref.shape
    width = feat_hbm.shape[1]
    copies = [
        pltpu.make_async_copy(owners_hbm, owners_ref, sems.at[0]),
        pltpu.make_async_copy(clusters_hbm, clusters_ref, sems.at[1]),
        pltpu.make_async_copy(feat_hbm, rows_ref.at[0], sems.at[2]),
        pltpu.make_async_copy(grad_hbm, rows_ref.at[1], sems.at[3]),
    ]
    for copy in copies:
        copy.start()
    acc_ref[...] = jnp.zeros_like(acc_ref)
    for copy in copies:
        copy.wait()
    token = lax.broadcasted_iota(jnp.int32, (t_rows, rows), 0)
    for b in range(blocks):
        member = (clusters_ref[b : b + 1, :] == token).astype(F32)
        span = pl.ds(b * rows, rows)
        both = jnp.concatenate([rows_ref[0, span, :], rows_ref[1, span, :]], axis=1)
        sums = jnp.dot(member.astype(BF16), both, preferred_element_type=F32)
        place = pl.ds(pl.multiple_of(owners_ref[b] * t_rows, t_rows), t_rows)
        acc_ref[place, : 2 * width] += sums
        acc_ref[place, 2 * width :] += member
    me = lax.axis_index("shard")
    for k in range(pairs):
        mine = me ^ chip(k)
        keep_ref[k] = acc_ref[pl.ds(pl.multiple_of(mine * t_rows, t_rows), t_rows), :]
        other = mine ^ 1
        give_ref[k] = acc_ref[pl.ds(pl.multiple_of(other * t_rows, t_rows), t_rows), :].astype(BF16)


def pool(particles, cotangent, clusters, owners, t_rows, n_shard):
    num_blocks = owners.shape[0]
    count, width = particles.shape
    rows = count // num_blocks
    shape = (n_shard // 2, t_rows, 2 * width + rows)
    whole = pl.BlockSpec(memory_space=pl.ANY)
    return pl.pallas_call(
        pool_kernel,
        in_specs=[whole] * 4,
        out_specs=[VMEM, VMEM],
        out_shape=[jax.ShapeDtypeStruct(shape, F32), jax.ShapeDtypeStruct(shape, BF16)],
        scratch_shapes=[
            pltpu.VMEM((n_shard * t_rows, shape[2]), F32),
            pltpu.VMEM((2, count, width), BF16),
            pltpu.SemaphoreType.DMA((4,)),
            pltpu.SMEM(owners.shape, jnp.int32),
            pltpu.VMEM((num_blocks, rows), jnp.int32),
        ],
        compiler_params=params(60),
        name="pool",
    )(owners, clusters.reshape(num_blocks, rows), particles, cotangent)


def attend_kernel(parts, *refs):
    tok, pooled_refs = refs[:parts], refs[parts : 2 * parts]
    near, far, w_in, w_out, up_ref, keep_ref, give_ref, weight, hid, term = refs[2 * parts :]
    pairs, rows, cols = near.shape
    t_rows, width = tok[0].shape
    head_cols = cols * parts
    channels = w_in.shape[0]
    group, me = lax.axis_index("group"), lax.axis_index("shard")
    part = lax.rem(group, parts)
    core = lax.rem(me, 2)
    pair = lax.div(me, 2)
    for k in range(pairs):
        mine = me ^ chip(reverse(k, pairs))
        weight[pl.ds(pl.multiple_of(mine * rows, rows), rows), :] = near[k]
        weight[pl.ds(pl.multiple_of((mine ^ 1) * rows, rows), rows), :] = far[k]
    pooled = jnp.concatenate([r[:, :channels] for r in pooled_refs], axis=0)
    pooled_grad = jnp.concatenate([r[:, channels:] for r in pooled_refs], axis=0)
    step = 512
    for n in range(0, width, step):
        wide = jnp.dot(pooled, w_in[:, n : n + step], preferred_element_type=F32)
        for k in range(parts):
            span = slice(k * t_rows, (k + 1) * t_rows)
            hid[span, n : n + step] = (
                tok[k][:, n : n + step].astype(F32) + wide[span]
            ).astype(BF16)
    queries = jnp.dot(hid[...], weight[...], preferred_element_type=F32).astype(BF16)
    first = pl.ds(pl.multiple_of(part * cols, cols), cols)
    values = hid[:, first]
    out_w = w_out[first, :]
    out_grad = contract(pooled_grad, out_w, 1, 1).astype(BF16)
    dim = head_cols // HEADS
    scale = 1.0 / math.sqrt(dim)
    total = parts * t_rows
    row = lax.broadcasted_iota(jnp.int32, (total, total), 0)
    col = lax.broadcasted_iota(jnp.int32, (total, total), 1)
    same = lax.div(row, t_rows) == lax.div(col, t_rows)
    outs, grads = [], []
    for h in range(cols // dim):
        lanes = slice(h * dim, (h + 1) * dim)
        q, v, g = queries[:, lanes], values[:, lanes], out_grad[:, lanes]
        scores = contract(q, q, 1, 1) * scale
        scores = jnp.where(row == col, -1000000000.0, scores)
        scores = jnp.where(same, scores, -3.0e38)
        e = jnp.exp(scores - jnp.max(scores, axis=1, keepdims=True))
        prob = e / jnp.sum(e, axis=1, keepdims=True)
        attended = jnp.dot(prob.astype(BF16), v, preferred_element_type=F32)
        outs.append((v.astype(F32) + attended).astype(BF16))
        prob_grad = contract(g, v, 1, 1)
        inner = jnp.sum(prob_grad * prob, axis=1, keepdims=True)
        score_grad = (prob * (prob_grad - inner) * scale).astype(BF16)
        grads.append(
            jnp.dot(score_grad, q, preferred_element_type=F32) + contract(score_grad, q, 0, 0)
        )
    output = jnp.concatenate(outs, axis=1)
    q_grad = jnp.concatenate(grads, axis=1).astype(BF16)
    rest = (width - head_cols) // parts
    second = pl.ds(pl.multiple_of(head_cols + part * rest, rest), rest)
    up = jnp.dot(output, out_w, preferred_element_type=F32) + jnp.dot(
        hid[:, second], w_out[second, :], preferred_element_type=F32
    )
    for k in range(parts):
        up_ref[k] = up[k * t_rows : (k + 1) * t_rows].astype(BF16)
    for k in range(pairs):
        chunk = pl.ds(pl.multiple_of((pair ^ k) * (2 * rows), 2 * rows), 2 * rows)
        term[...] = contract(hid[:, chunk], q_grad, 0, 0)
        mine = core ^ odd(k)
        keep_ref[k] = term[pl.ds(pl.multiple_of(mine * rows, rows), rows), :].astype(BF16)
        give_ref[k] = term[pl.ds(pl.multiple_of((1 - mine) * rows, rows), rows), :].astype(BF16)


def attend(tok, pooled, near, far, w_in, w_out):
    parts = len(tok)
    t_rows, width = tok[0].shape
    pairs, rows, cols = near.shape
    channels = w_in.shape[0]
    shape = jax.ShapeDtypeStruct((pairs, rows, cols), BF16)
    return pl.pallas_call(
        functools.partial(attend_kernel, parts),
        in_specs=[VMEM] * (2 * parts + 4),
        out_specs=[VMEM] * 3,
        out_shape=[jax.ShapeDtypeStruct((parts, t_rows, channels), BF16), shape, shape],
        scratch_shapes=[
            pltpu.VMEM((width, cols), BF16),
            pltpu.VMEM((parts * t_rows, width), BF16),
            pltpu.VMEM((2 * rows, cols), F32),
        ],
        compiler_params=params(24),
        name="attend",
    )(*tok, *pooled, near, far, w_in, w_out)


def unpool_kernel(owners_ref, clusters_ref, feat_ref, near, far, out_ref, rows_ref):
    step = pl.program_id(0)
    blocks, rows = clusters_ref.shape
    pairs, t_rows, _ = near.shape

    @pl.when(step == 0)
    def _():
        me = lax.axis_index("shard")
        for k in range(pairs):
            mine = me ^ chip(k)
            rows_ref[pl.ds(pl.multiple_of(mine * t_rows, t_rows), t_rows), :] = near[k]
            rows_ref[pl.ds(pl.multiple_of((mine ^ 1) * t_rows, t_rows), t_rows), :] = far[k]

    token = lax.broadcasted_iota(jnp.int32, (t_rows, rows), 0)
    for b in range(blocks):
        member = (clusters_ref[b : b + 1, :] == token).astype(F32).astype(BF16)
        place = pl.ds(pl.multiple_of(owners_ref[step * blocks + b] * t_rows, t_rows), t_rows)
        span = pl.ds(b * rows, rows)
        picked = contract(member, rows_ref[place, :], 0, 0)
        out_ref[span, :] = (feat_ref[span, :].astype(F32) + picked).astype(BF16)


def unpool(particles, clusters, owners, near, far):
    num_blocks = owners.shape[0]
    count, width = particles.shape
    rows = count // num_blocks
    steps = 4
    pairs, t_rows, _ = near.shape
    whole = pl.BlockSpec(near.shape, lambda i, own: (0, 0, 0))
    return pl.pallas_call(
        unpool_kernel,
        grid_spec=pltpu.PrefetchScalarGridSpec(
            num_scalar_prefetch=1,
            grid=(steps,),
            in_specs=[
                pl.BlockSpec((num_blocks // steps, rows), lambda i, own: (i, 0)),
                pl.BlockSpec((count // steps, width), lambda i, own: (i, 0)),
                whole,
                whole,
            ],
            out_specs=pl.BlockSpec((count // steps, width), lambda i, own: (i, 0)),
            scratch_shapes=[pltpu.VMEM((2 * pairs * t_rows, width), BF16)],
        ),
        out_shape=jax.ShapeDtypeStruct(particles.shape, BF16),
        compiler_params=params(16),
        name="unpool",
    )(owners, clusters.reshape(num_blocks, rows), particles, near, far)


def spread_kernel(*refs):
    pieces, out_ref = refs[:-1], refs[-1]
    part = lax.rem(lax.axis_index("group"), len(pieces))
    cols = pieces[0].shape[1]
    for k, piece in enumerate(pieces):
        out_ref[:, pl.ds(pl.multiple_of((part ^ k) * cols, cols), cols)] = piece[...].astype(F32)


def spread(pieces):
    rows, cols = pieces[0].shape
    return pl.pallas_call(
        spread_kernel,
        in_specs=[VMEM] * len(pieces),
        out_specs=VMEM,
        out_shape=jax.ShapeDtypeStruct((rows, cols * len(pieces)), F32),
        compiler_params=params(16),
        name="spread",
    )(*pieces)


def swap(x, group, shard):
    n = lax.axis_size("shard")
    flip = group * n + shard
    pairs = [(i, i ^ flip) for i in range(lax.axis_size("group") * n)]
    return lax.ppermute(x, ("group", "shard"), pairs)


def odd(k):
    return bin(k).count("1") % 2


def reverse(k, count):
    bits = count.bit_length() - 1
    return sum(((k >> i) & 1) << (bits - 1 - i) for i in range(bits))


def chip(k):
    return 2 * k + odd(k)


def local(tokens, w_qk, w_in, w_out, particles, cotangent, clusters, owners):
    n_group, n_shard = lax.axis_size("group"), lax.axis_size("shard")
    parts = math.gcd(n_group, 4)
    pairs = n_shard // 2
    t_rows = tokens.shape[0]
    cols = w_qk.shape[1] // parts
    part = lax.rem(lax.axis_index("group"), parts)

    w_own = lax.dynamic_slice_in_dim(w_qk, part * cols, cols, axis=1)

    bits = [pairs >> i for i in range(1, pairs.bit_length())]
    first = [w_own[None]]
    for k in bits[:-1]:
        first.append(swap(jnp.concatenate(first), 0, chip(k)))
    tok = tokens[None]
    tok_x = swap(tok, 1, 1)
    tok = jnp.concatenate([tok, tok_x])
    for k in [1 << i for i in range(1, parts.bit_length() - 1)]:
        tok = jnp.concatenate([tok, swap(tok, k, 1)])

    keep, give = pool(particles, cotangent, clusters, owners, t_rows, n_shard)
    got = swap(give, 0, 1)
    got, first[-1], tok_x = lax.optimization_barrier((got, first[-1], tok_x))
    first = jnp.concatenate(first)
    joined = keep + got.astype(F32)
    sums = joined[0]
    for k in range(1, pairs):
        sums = sums + swap(joined[k].astype(BF16), 0, chip(k)).astype(F32)
    second = swap(first, 0, chip(1))
    far_first = swap(first, 0, 1)
    channels = particles.shape[1]
    counts = jnp.sum(sums[:, 2 * channels :], axis=1, keepdims=True)
    pooled = jnp.concatenate(
        [sums[:, :channels] / jnp.maximum(counts, 1.0), sums[:, channels : 2 * channels]], axis=1
    ).astype(BF16)
    pooled = [pooled] + [swap(pooled, k, odd(k)) for k in range(1, parts)]
    second, pooled[-1] = lax.optimization_barrier((second, pooled[-1]))
    near = jnp.concatenate([first, second])
    far = jnp.concatenate([far_first, swap(second, 0, 1)])

    up, keep, give = attend([tok[0], tok_x[0]] + [tok[k] for k in range(2, parts)], pooled, near, far, w_in, w_out)

    joined = keep.astype(F32) + swap(give, 0, 1).astype(F32)
    unpooled = up[0].astype(F32)
    for k in range(1, parts):
        unpooled = unpooled + swap(up[k], k, odd(k)).astype(F32)
    unpooled = unpooled.astype(BF16)
    near = jnp.stack([unpooled] + [swap(unpooled, 0, chip(k)) for k in range(1, pairs)])
    far = swap(near, 0, 1)
    particle_out = unpool(particles, clusters, owners, near, far)

    grad = joined[0]
    for k in range(1, pairs):
        grad = grad + swap(joined[k].astype(BF16), 0, chip(k)).astype(F32)
    if n_group > parts:
        part_sum = grad.astype(BF16)
        for k in range(1, n_group // parts):
            grad = grad + swap(part_sum, k * parts, 0).astype(F32)
    grad = grad.astype(BF16)
    qk_grad = spread([grad] + [swap(grad, k, 0) for k in range(1, parts)])
    return (particle_out, qk_grad)


def solution(mesh):
    placed = (
        P(("group", "shard"), None),
        P("shard", None),
        P(),
        P(),
        P(("group", "shard"), None),
        P(("group", "shard"), None),
        P(("group", "shard")),
        P(("group", "shard")),
    )
    return jax.shard_map(
        local,
        mesh=mesh,
        in_specs=placed,
        out_specs=(P(("group", "shard"), None), P("shard", None)),
        check_vma=False,
    )
```

```python
import functools
import math

import jax
import jax.numpy as jnp
from jax import lax
from jax.experimental import pallas as pl
from jax.experimental.pallas import tpu as pltpu
from jax.sharding import PartitionSpec as P

HEADS = 8
F32 = jnp.float32
BF16 = jnp.bfloat16
VMEM = pl.BlockSpec(memory_space=pltpu.VMEM)


def params(mib):
    return pltpu.CompilerParams(vmem_limit_bytes=mib << 20)


def contract(a, b, da, db):
    return lax.dot_general(a, b, (((da,), (db,)), ((), ())), preferred_element_type=F32)


def pool_kernel(
    owners_hbm, clusters_hbm, feat_hbm, grad_hbm, keep_ref, give_ref, acc_ref, rows_ref, sems, owners_ref, clusters_ref
):
    blocks, rows = clusters_ref.shape
    pairs, t_rows, _ = keep_ref.shape
    width = feat_hbm.shape[1]
    copies = [
        pltpu.make_async_copy(owners_hbm, owners_ref, sems.at[0]),
        pltpu.make_async_copy(clusters_hbm, clusters_ref, sems.at[1]),
        pltpu.make_async_copy(feat_hbm, rows_ref.at[0], sems.at[2]),
        pltpu.make_async_copy(grad_hbm, rows_ref.at[1], sems.at[3]),
    ]
    for copy in copies:
        copy.start()
    acc_ref[...] = jnp.zeros_like(acc_ref)
    for copy in copies:
        copy.wait()
    token = lax.broadcasted_iota(jnp.int32, (t_rows, rows), 0)
    for b in range(blocks):
        member = (clusters_ref[b : b + 1, :] == token).astype(F32)
        span = pl.ds(b * rows, rows)
        both = jnp.concatenate([rows_ref[0, span, :], rows_ref[1, span, :]], axis=1)
        sums = jnp.dot(member.astype(BF16), both, preferred_element_type=F32)
        place = pl.ds(pl.multiple_of(owners_ref[b] * t_rows, t_rows), t_rows)
        acc_ref[place, : 2 * width] += sums
        acc_ref[place, 2 * width :] += member
    me = lax.axis_index("shard")
    for k in range(pairs):
        mine = me ^ chip(k)
        keep_ref[k] = acc_ref[pl.ds(pl.multiple_of(mine * t_rows, t_rows), t_rows), :]
        other = mine ^ 1
        give_ref[k] = acc_ref[pl.ds(pl.multiple_of(other * t_rows, t_rows), t_rows), :].astype(BF16)


def pool(particles, cotangent, clusters, owners, t_rows, n_shard):
    num_blocks = owners.shape[0]
    count, width = particles.shape
    rows = count // num_blocks
    shape = (n_shard // 2, t_rows, 2 * width + rows)
    whole = pl.BlockSpec(memory_space=pl.ANY)
    return pl.pallas_call(
        pool_kernel,
        in_specs=[whole] * 4,
        out_specs=[VMEM, VMEM],
        out_shape=[jax.ShapeDtypeStruct(shape, F32), jax.ShapeDtypeStruct(shape, BF16)],
        scratch_shapes=[
            pltpu.VMEM((n_shard * t_rows, shape[2]), F32),
            pltpu.VMEM((2, count, width), BF16),
            pltpu.SemaphoreType.DMA((4,)),
            pltpu.SMEM(owners.shape, jnp.int32),
            pltpu.VMEM((num_blocks, rows), jnp.int32),
        ],
        compiler_params=params(60),
        name="pool",
    )(owners, clusters.reshape(num_blocks, rows), particles, cotangent)


def attend_kernel(parts, *refs):
    tok, pooled_refs = refs[:parts], refs[parts : 2 * parts]
    near, far, w_in, w_out, up_ref, keep_ref, give_ref, weight, hid, term = refs[2 * parts :]
    pairs, rows, cols = near.shape
    t_rows, width = tok[0].shape
    head_cols = cols * parts
    channels = w_in.shape[0]
    group, me = lax.axis_index("group"), lax.axis_index("shard")
    part = lax.rem(group, parts)
    core = lax.rem(me, 2)
    pair = lax.div(me, 2)
    for k in range(pairs):
        mine = me ^ chip(reverse(k, pairs))
        weight[pl.ds(pl.multiple_of(mine * rows, rows), rows), :] = near[k]
        weight[pl.ds(pl.multiple_of((mine ^ 1) * rows, rows), rows), :] = far[k]
    pooled = jnp.concatenate([r[:, :channels] for r in pooled_refs], axis=0)
    pooled_grad = jnp.concatenate([r[:, channels:] for r in pooled_refs], axis=0)
    step = 512
    for n in range(0, width, step):
        wide = jnp.dot(pooled, w_in[:, n : n + step], preferred_element_type=F32)
        for k in range(parts):
            span = slice(k * t_rows, (k + 1) * t_rows)
            hid[span, n : n + step] = (
                tok[k][:, n : n + step].astype(F32) + wide[span]
            ).astype(BF16)
    queries = jnp.dot(hid[...], weight[...], preferred_element_type=F32).astype(BF16)
    first = pl.ds(pl.multiple_of(part * cols, cols), cols)
    values = hid[:, first]
    out_w = w_out[first, :]
    out_grad = contract(pooled_grad, out_w, 1, 1).astype(BF16)
    dim = head_cols // HEADS
    scale = 1.0 / math.sqrt(dim)
    total = parts * t_rows
    row = lax.broadcasted_iota(jnp.int32, (total, total), 0)
    col = lax.broadcasted_iota(jnp.int32, (total, total), 1)
    same = lax.div(row, t_rows) == lax.div(col, t_rows)
    outs, grads = [], []
    for h in range(cols // dim):
        lanes = slice(h * dim, (h + 1) * dim)
        q, v, g = queries[:, lanes], values[:, lanes], out_grad[:, lanes]
        scores = contract(q, q, 1, 1) * scale
        scores = jnp.where(row == col, -1000000000.0, scores)
        scores = jnp.where(same, scores, -3.0e38)
        e = jnp.exp(scores - jnp.max(scores, axis=1, keepdims=True))
        prob = e / jnp.sum(e, axis=1, keepdims=True)
        attended = jnp.dot(prob.astype(BF16), v, preferred_element_type=F32)
        outs.append((v.astype(F32) + attended).astype(BF16))
        prob_grad = contract(g, v, 1, 1)
        inner = jnp.sum(prob_grad * prob, axis=1, keepdims=True)
        score_grad = (prob * (prob_grad - inner) * scale).astype(BF16)
        grads.append(
            jnp.dot(score_grad, q, preferred_element_type=F32) + contract(score_grad, q, 0, 0)
        )
    output = jnp.concatenate(outs, axis=1)
    q_grad = jnp.concatenate(grads, axis=1).astype(BF16)
    rest = (width - head_cols) // parts
    second = pl.ds(pl.multiple_of(head_cols + part * rest, rest), rest)
    up = jnp.dot(output, out_w, preferred_element_type=F32) + jnp.dot(
        hid[:, second], w_out[second, :], preferred_element_type=F32
    )
    for k in range(parts):
        up_ref[k] = up[k * t_rows : (k + 1) * t_rows].astype(BF16)
    for k in range(pairs):
        chunk = pl.ds(pl.multiple_of((pair ^ k) * (2 * rows), 2 * rows), 2 * rows)
        term[...] = contract(hid[:, chunk], q_grad, 0, 0)
        mine = 1 ^ core ^ odd(k)
        keep_ref[k] = term[pl.ds(pl.multiple_of(mine * rows, rows), rows), :].astype(BF16)
        give_ref[k] = term[pl.ds(pl.multiple_of((1 - mine) * rows, rows), rows), :].astype(BF16)


def attend(tok, pooled, near, far, w_in, w_out):
    parts = len(tok)
    t_rows, width = tok[0].shape
    pairs, rows, cols = near.shape
    channels = w_in.shape[0]
    shape = jax.ShapeDtypeStruct((pairs, rows, cols), BF16)
    return pl.pallas_call(
        functools.partial(attend_kernel, parts),
        in_specs=[VMEM] * (2 * parts + 4),
        out_specs=[VMEM] * 3,
        out_shape=[jax.ShapeDtypeStruct((parts, t_rows, channels), BF16), shape, shape],
        scratch_shapes=[
            pltpu.VMEM((width, cols), BF16),
            pltpu.VMEM((parts * t_rows, width), BF16),
            pltpu.VMEM((2 * rows, cols), F32),
        ],
        compiler_params=params(24),
        name="attend",
    )(*tok, *pooled, near, far, w_in, w_out)


def unpool_kernel(owners_ref, clusters_ref, feat_ref, near, far, out_ref, rows_ref):
    step = pl.program_id(0)
    blocks, rows = clusters_ref.shape
    pairs, t_rows, _ = near.shape

    @pl.when(step == 0)
    def _():
        me = lax.axis_index("shard")
        for k in range(pairs):
            mine = me ^ chip(k)
            rows_ref[pl.ds(pl.multiple_of(mine * t_rows, t_rows), t_rows), :] = near[k]
            rows_ref[pl.ds(pl.multiple_of((mine ^ 1) * t_rows, t_rows), t_rows), :] = far[k]

    token = lax.broadcasted_iota(jnp.int32, (t_rows, rows), 0)
    for b in range(blocks):
        member = (clusters_ref[b : b + 1, :] == token).astype(F32).astype(BF16)
        place = pl.ds(pl.multiple_of(owners_ref[step * blocks + b] * t_rows, t_rows), t_rows)
        span = pl.ds(b * rows, rows)
        picked = contract(member, rows_ref[place, :], 0, 0)
        out_ref[span, :] = (feat_ref[span, :].astype(F32) + picked).astype(BF16)


def unpool(particles, clusters, owners, near, far):
    num_blocks = owners.shape[0]
    count, width = particles.shape
    rows = count // num_blocks
    steps = 4
    pairs, t_rows, _ = near.shape
    whole = pl.BlockSpec(near.shape, lambda i, own: (0, 0, 0))
    return pl.pallas_call(
        unpool_kernel,
        grid_spec=pltpu.PrefetchScalarGridSpec(
            num_scalar_prefetch=1,
            grid=(steps,),
            in_specs=[
                pl.BlockSpec((num_blocks // steps, rows), lambda i, own: (i, 0)),
                pl.BlockSpec((count // steps, width), lambda i, own: (i, 0)),
                whole,
                whole,
            ],
            out_specs=pl.BlockSpec((count // steps, width), lambda i, own: (i, 0)),
            scratch_shapes=[pltpu.VMEM((2 * pairs * t_rows, width), BF16)],
        ),
        out_shape=jax.ShapeDtypeStruct(particles.shape, BF16),
        compiler_params=params(16),
        name="unpool",
    )(owners, clusters.reshape(num_blocks, rows), particles, near, far)


def spread_kernel(*refs):
    pieces, out_ref = refs[:-1], refs[-1]
    part = lax.rem(lax.axis_index("group"), len(pieces))
    cols = pieces[0].shape[1]
    for k, piece in enumerate(pieces):
        out_ref[:, pl.ds(pl.multiple_of((part ^ k) * cols, cols), cols)] = piece[...].astype(F32)


def spread(pieces):
    rows, cols = pieces[0].shape
    return pl.pallas_call(
        spread_kernel,
        in_specs=[VMEM] * len(pieces),
        out_specs=VMEM,
        out_shape=jax.ShapeDtypeStruct((rows, cols * len(pieces)), F32),
        compiler_params=params(16),
        name="spread",
    )(*pieces)


def swap(x, group, shard):
    n = lax.axis_size("shard")
    flip = group * n + shard
    pairs = [(i, i ^ flip) for i in range(lax.axis_size("group") * n)]
    return lax.ppermute(x, ("group", "shard"), pairs)


def odd(k):
    return bin(k).count("1") % 2


def reverse(k, count):
    bits = count.bit_length() - 1
    return sum(((k >> i) & 1) << (bits - 1 - i) for i in range(bits))


def chip(k):
    return 2 * k + odd(k)


def local(tokens, w_qk, w_in, w_out, particles, cotangent, clusters, owners):
    n_group, n_shard = lax.axis_size("group"), lax.axis_size("shard")
    parts = math.gcd(n_group, 4)
    pairs = n_shard // 2
    t_rows = tokens.shape[0]
    cols = w_qk.shape[1] // parts
    part = lax.rem(lax.axis_index("group"), parts)

    w_own = lax.dynamic_slice_in_dim(w_qk, part * cols, cols, axis=1)

    bits = [pairs >> i for i in range(1, pairs.bit_length())]
    first = [w_own[None]]
    for k in bits[:-1]:
        first.append(swap(jnp.concatenate(first), 0, chip(k)))
    tok = tokens[None]
    tok_x = swap(tok, 1, 1)
    tok = jnp.concatenate([tok, tok_x])
    for k in [1 << i for i in range(1, parts.bit_length() - 1)]:
        tok = jnp.concatenate([tok, swap(tok, k, 1)])

    keep, give = pool(particles, cotangent, clusters, owners, t_rows, n_shard)
    got = swap(give, 0, 1)
    got, first[-1], tok_x = lax.optimization_barrier((got, first[-1], tok_x))
    first = jnp.concatenate(first)
    joined = keep + got.astype(F32)
    sums = joined[0]
    for k in [2, 1, *range(3, pairs)]:
        sums = sums + swap(joined[k].astype(BF16), 0, chip(k)).astype(F32)
    second = swap(first, 0, chip(1))
    far_first = swap(first, 0, 1)
    channels = particles.shape[1]
    counts = jnp.sum(sums[:, 2 * channels :], axis=1, keepdims=True)
    pooled = jnp.concatenate(
        [sums[:, :channels] / jnp.maximum(counts, 1.0), sums[:, channels : 2 * channels]], axis=1
    ).astype(BF16)
    pooled = [pooled] + [swap(pooled, k, odd(k)) for k in range(1, parts)]
    second, pooled = lax.optimization_barrier((second, pooled))
    near = jnp.concatenate([first, second])
    far = jnp.concatenate([far_first, swap(second, 0, 1)])

    up, keep, give = attend([tok[0], tok_x[0]] + [tok[k] for k in range(2, parts)], pooled, near, far, w_in, w_out)

    joined = keep.astype(F32) + swap(give, 0, 1).astype(F32)
    unpooled = up[0].astype(F32)
    for k in range(1, parts):
        unpooled = unpooled + swap(up[k], k, odd(k)).astype(F32)
    near = unpooled.astype(BF16)[None]
    for k in [1 << i for i in range(pairs.bit_length() - 1)]:
        near = jnp.concatenate([near, swap(near, 0, chip(k))])
    far = swap(near, 0, 1)
    particle_out = unpool(particles, clusters, owners, near, far)

    grad = joined[0]
    for k in [pairs - 1, *range(1, pairs - 1)]:
        grad = grad + swap(joined[k].astype(BF16), 0, chip(k)).astype(F32)
    if n_group > parts:
        part_sum = grad.astype(BF16)
        for k in range(1, n_group // parts):
            grad = grad + swap(part_sum, k * parts, 0).astype(F32)
    grad = grad.astype(BF16)
    qk_grad = spread([swap(grad, k, 1) for k in range(parts)])
    return (particle_out, qk_grad)


def solution(mesh):
    placed = (
        P(("group", "shard"), None),
        P("shard", None),
        P(),
        P(),
        P(("group", "shard"), None),
        P(("group", "shard"), None),
        P(("group", "shard")),
        P(("group", "shard")),
    )
    return jax.shard_map(
        local,
        mesh=mesh,
        in_specs=placed,
        out_specs=(P(("group", "shard"), None), P("shard", None)),
        check_vma=False,
    )
```

```python
import functools
import math

import jax
import jax.numpy as jnp
from jax import lax
from jax.experimental import pallas as pl
from jax.experimental.pallas import tpu as pltpu
from jax.sharding import PartitionSpec as P

HEADS = 8
F32 = jnp.float32
BF16 = jnp.bfloat16
VMEM = pl.BlockSpec(memory_space=pltpu.VMEM)


def params(mib):
    return pltpu.CompilerParams(vmem_limit_bytes=mib << 20)


def contract(a, b, da, db):
    return lax.dot_general(a, b, (((da,), (db,)), ((), ())), preferred_element_type=F32)


def pool_kernel(
    owners_hbm, clusters_hbm, feat_hbm, grad_hbm, keep_ref, give_ref, acc_ref, rows_ref, sems, owners_ref, clusters_ref
):
    blocks, rows = clusters_ref.shape
    pairs, t_rows, _ = keep_ref.shape
    width = feat_hbm.shape[1]
    copies = [
        pltpu.make_async_copy(owners_hbm, owners_ref, sems.at[0]),
        pltpu.make_async_copy(clusters_hbm, clusters_ref, sems.at[1]),
        pltpu.make_async_copy(feat_hbm, rows_ref.at[0], sems.at[2]),
        pltpu.make_async_copy(grad_hbm, rows_ref.at[1], sems.at[3]),
    ]
    for copy in copies:
        copy.start()
    acc_ref[...] = jnp.zeros_like(acc_ref)
    for copy in copies:
        copy.wait()
    token = lax.broadcasted_iota(jnp.int32, (t_rows, rows), 0)
    for b in range(blocks):
        member = (clusters_ref[b : b + 1, :] == token).astype(F32)
        span = pl.ds(b * rows, rows)
        both = jnp.concatenate([rows_ref[0, span, :], rows_ref[1, span, :]], axis=1)
        sums = jnp.dot(member.astype(BF16), both, preferred_element_type=F32)
        place = pl.ds(pl.multiple_of(owners_ref[b] * t_rows, t_rows), t_rows)
        acc_ref[place, : 2 * width] += sums
        acc_ref[place, 2 * width :] += member
    me = lax.axis_index("shard")
    for k in range(pairs):
        mine = me ^ chip(k)
        keep_ref[k] = acc_ref[pl.ds(pl.multiple_of(mine * t_rows, t_rows), t_rows), :]
        other = mine ^ 1
        give_ref[k] = acc_ref[pl.ds(pl.multiple_of(other * t_rows, t_rows), t_rows), :].astype(BF16)


def pool(particles, cotangent, clusters, owners, t_rows, n_shard):
    num_blocks = owners.shape[0]
    count, width = particles.shape
    rows = count // num_blocks
    shape = (n_shard // 2, t_rows, 2 * width + rows)
    whole = pl.BlockSpec(memory_space=pl.ANY)
    return pl.pallas_call(
        pool_kernel,
        in_specs=[whole] * 4,
        out_specs=[VMEM, VMEM],
        out_shape=[jax.ShapeDtypeStruct(shape, F32), jax.ShapeDtypeStruct(shape, BF16)],
        scratch_shapes=[
            pltpu.VMEM((n_shard * t_rows, shape[2]), F32),
            pltpu.VMEM((2, count, width), BF16),
            pltpu.SemaphoreType.DMA((4,)),
            pltpu.SMEM(owners.shape, jnp.int32),
            pltpu.VMEM((num_blocks, rows), jnp.int32),
        ],
        compiler_params=params(60),
        name="pool",
    )(owners, clusters.reshape(num_blocks, rows), particles, cotangent)


def query_part(hid, near, far, pairs, begin, weight):
    me = lax.axis_index("shard")
    count, rows, _ = near.shape
    total = None
    for i in range(count):
        mine = me ^ chip(reverse(begin + i, pairs))
        core = lax.rem(mine, 2)
        weight[i, pl.ds(pl.multiple_of(core * rows, rows), rows), :] = near[i]
        weight[i, pl.ds(pl.multiple_of((1 - core) * rows, rows), rows), :] = far[i]
        chunk = pl.ds(pl.multiple_of(lax.div(mine, 2) * (2 * rows), 2 * rows), 2 * rows)
        term = jnp.dot(hid[:, chunk], weight[i], preferred_element_type=F32)
        total = term if total is None else total + term
    return total


def hidden_kernel(parts, *refs):
    tok, pooled_refs = refs[:parts], refs[parts : 2 * parts]
    near, far, w_in, hid, query, weight = refs[2 * parts :]
    t_rows, width = tok[0].shape
    channels = w_in.shape[0]
    pooled = jnp.concatenate([r[:, :channels] for r in pooled_refs], axis=0)
    step = 512
    for n in range(0, width, step):
        wide = jnp.dot(pooled, w_in[:, n : n + step], preferred_element_type=F32)
        for k in range(parts):
            span = slice(k * t_rows, (k + 1) * t_rows)
            hid[span, n : n + step] = (
                tok[k][:, n : n + step].astype(F32) + wide[span]
            ).astype(BF16)
    query[...] = query_part(hid, near, far, 2 * near.shape[0], 0, weight)


def hidden(tok, pooled, near, far, w_in):
    parts = len(tok)
    t_rows, width = tok[0].shape
    half, rows, cols = near.shape
    return pl.pallas_call(
        functools.partial(hidden_kernel, parts),
        in_specs=[VMEM] * (2 * parts + 3),
        out_specs=[VMEM] * 2,
        out_shape=[
            jax.ShapeDtypeStruct((parts * t_rows, width), BF16),
            jax.ShapeDtypeStruct((parts * t_rows, cols), F32),
        ],
        scratch_shapes=[pltpu.VMEM((half, 2 * rows, cols), BF16)],
        compiler_params=params(20),
        name="hidden",
    )(*tok, *pooled, near, far, w_in)


def attend_kernel(parts, *refs):
    pooled_refs = refs[:parts]
    hid, query, near, far, w_out, up_ref, keep_ref, give_ref, weight, term = refs[parts:]
    half_pairs, rows, cols = near.shape
    pairs = 2 * half_pairs
    total, width = hid.shape
    t_rows = total // parts
    head_cols = cols * parts
    channels = w_out.shape[1]
    group, me = lax.axis_index("group"), lax.axis_index("shard")
    part = lax.rem(group, parts)
    core = lax.rem(me, 2)
    pair = lax.div(me, 2)
    queries = (query[...] + query_part(hid, near, far, pairs, half_pairs, weight)).astype(BF16)
    pooled_grad = jnp.concatenate([r[:, channels:] for r in pooled_refs], axis=0)
    first = pl.ds(pl.multiple_of(part * cols, cols), cols)
    values = hid[:, first]
    out_w = w_out[first, :]
    out_grad = contract(pooled_grad, out_w, 1, 1).astype(BF16)
    dim = head_cols // HEADS
    scale = 1.0 / math.sqrt(dim)
    row = lax.broadcasted_iota(jnp.int32, (total, total), 0)
    col = lax.broadcasted_iota(jnp.int32, (total, total), 1)
    same = lax.div(row, t_rows) == lax.div(col, t_rows)
    outs, grads = [], []
    for h in range(cols // dim):
        lanes = slice(h * dim, (h + 1) * dim)
        q, v, g = queries[:, lanes], values[:, lanes], out_grad[:, lanes]
        scores = contract(q, q, 1, 1) * scale
        scores = jnp.where(row == col, -1000000000.0, scores)
        scores = jnp.where(same, scores, -3.0e38)
        e = jnp.exp(scores - jnp.max(scores, axis=1, keepdims=True))
        prob = e / jnp.sum(e, axis=1, keepdims=True)
        attended = jnp.dot(prob.astype(BF16), v, preferred_element_type=F32)
        outs.append((v.astype(F32) + attended).astype(BF16))
        prob_grad = contract(g, v, 1, 1)
        inner = jnp.sum(prob_grad * prob, axis=1, keepdims=True)
        score_grad = (prob * (prob_grad - inner) * scale).astype(BF16)
        grads.append(
            jnp.dot(score_grad, q, preferred_element_type=F32) + contract(score_grad, q, 0, 0)
        )
    output = jnp.concatenate(outs, axis=1)
    q_grad = jnp.concatenate(grads, axis=1).astype(BF16)
    rest = (width - head_cols) // parts
    second = pl.ds(pl.multiple_of(head_cols + part * rest, rest), rest)
    up = jnp.dot(output, out_w, preferred_element_type=F32) + jnp.dot(
        hid[:, second], w_out[second, :], preferred_element_type=F32
    )
    for k in range(parts):
        up_ref[k] = up[k * t_rows : (k + 1) * t_rows].astype(BF16)
    for k in range(pairs):
        chunk = pl.ds(pl.multiple_of((pair ^ k) * (2 * rows), 2 * rows), 2 * rows)
        term[...] = contract(hid[:, chunk], q_grad, 0, 0)
        mine = 1 ^ core ^ odd(k)
        keep_ref[k] = term[pl.ds(pl.multiple_of(mine * rows, rows), rows), :].astype(BF16)
        give_ref[k] = term[pl.ds(pl.multiple_of((1 - mine) * rows, rows), rows), :].astype(BF16)


def attend(pooled, hid, query, near, far, w_out):
    parts = len(pooled)
    half, rows, cols = near.shape
    channels = w_out.shape[1]
    t_rows = pooled[0].shape[0]
    shape = jax.ShapeDtypeStruct((2 * half, rows, cols), BF16)
    return pl.pallas_call(
        functools.partial(attend_kernel, parts),
        in_specs=[VMEM] * (parts + 5),
        out_specs=[VMEM] * 3,
        out_shape=[jax.ShapeDtypeStruct((parts, t_rows, channels), BF16), shape, shape],
        scratch_shapes=[
            pltpu.VMEM((half, 2 * rows, cols), BF16),
            pltpu.VMEM((2 * rows, cols), F32),
        ],
        compiler_params=params(20),
        name="attend",
    )(*pooled, hid, query, near, far, w_out)


def unpool_kernel(owners_ref, clusters_ref, feat_ref, near, far, out_ref, rows_ref):
    step = pl.program_id(0)
    blocks, rows = clusters_ref.shape
    pairs, t_rows, _ = near.shape

    @pl.when(step == 0)
    def _():
        me = lax.axis_index("shard")
        for k in range(pairs):
            mine = me ^ chip(k)
            rows_ref[pl.ds(pl.multiple_of(mine * t_rows, t_rows), t_rows), :] = near[k]
            rows_ref[pl.ds(pl.multiple_of((mine ^ 1) * t_rows, t_rows), t_rows), :] = far[k]

    token = lax.broadcasted_iota(jnp.int32, (t_rows, rows), 0)
    for b in range(blocks):
        member = (clusters_ref[b : b + 1, :] == token).astype(F32).astype(BF16)
        place = pl.ds(pl.multiple_of(owners_ref[step * blocks + b] * t_rows, t_rows), t_rows)
        span = pl.ds(b * rows, rows)
        picked = contract(member, rows_ref[place, :], 0, 0)
        out_ref[span, :] = (feat_ref[span, :].astype(F32) + picked).astype(BF16)


def unpool(particles, clusters, owners, near, far):
    num_blocks = owners.shape[0]
    count, width = particles.shape
    rows = count // num_blocks
    steps = 4
    pairs, t_rows, _ = near.shape
    whole = pl.BlockSpec(near.shape, lambda i, own: (0, 0, 0))
    return pl.pallas_call(
        unpool_kernel,
        grid_spec=pltpu.PrefetchScalarGridSpec(
            num_scalar_prefetch=1,
            grid=(steps,),
            in_specs=[
                pl.BlockSpec((num_blocks // steps, rows), lambda i, own: (i, 0)),
                pl.BlockSpec((count // steps, width), lambda i, own: (i, 0)),
                whole,
                whole,
            ],
            out_specs=pl.BlockSpec((count // steps, width), lambda i, own: (i, 0)),
            scratch_shapes=[pltpu.VMEM((2 * pairs * t_rows, width), BF16)],
        ),
        out_shape=jax.ShapeDtypeStruct(particles.shape, BF16),
        compiler_params=params(16),
        name="unpool",
    )(owners, clusters.reshape(num_blocks, rows), particles, near, far)


def spread_kernel(*refs):
    pieces, out_ref = refs[:-1], refs[-1]
    part = lax.rem(lax.axis_index("group"), len(pieces))
    cols = pieces[0].shape[1]
    for k, piece in enumerate(pieces):
        out_ref[:, pl.ds(pl.multiple_of((part ^ k) * cols, cols), cols)] = piece[...].astype(F32)


def spread(pieces):
    rows, cols = pieces[0].shape
    return pl.pallas_call(
        spread_kernel,
        in_specs=[VMEM] * len(pieces),
        out_specs=VMEM,
        out_shape=jax.ShapeDtypeStruct((rows, cols * len(pieces)), F32),
        compiler_params=params(16),
        name="spread",
    )(*pieces)


def swap(x, group, shard):
    n = lax.axis_size("shard")
    flip = group * n + shard
    pairs = [(i, i ^ flip) for i in range(lax.axis_size("group") * n)]
    return lax.ppermute(x, ("group", "shard"), pairs)


def odd(k):
    return bin(k).count("1") % 2


def reverse(k, count):
    bits = count.bit_length() - 1
    return sum(((k >> i) & 1) << (bits - 1 - i) for i in range(bits))


def chip(k):
    return 2 * k + odd(k)


def local(tokens, w_qk, w_in, w_out, particles, cotangent, clusters, owners):
    n_group, n_shard = lax.axis_size("group"), lax.axis_size("shard")
    parts = math.gcd(n_group, 4)
    pairs = n_shard // 2
    t_rows = tokens.shape[0]
    cols = w_qk.shape[1] // parts
    part = lax.rem(lax.axis_index("group"), parts)

    w_own = lax.dynamic_slice_in_dim(w_qk, part * cols, cols, axis=1)

    bits = [pairs >> i for i in range(1, pairs.bit_length())]
    first = [w_own[None]]
    for k in bits[:-1]:
        first.append(swap(jnp.concatenate(first), 0, chip(k)))
    tok = tokens[None]
    tok_x = swap(tok, 1, 1)
    tok = jnp.concatenate([tok, tok_x])
    for k in [1 << i for i in range(1, parts.bit_length() - 1)]:
        tok = jnp.concatenate([tok, swap(tok, k, 1)])

    keep, give = pool(particles, cotangent, clusters, owners, t_rows, n_shard)
    got = swap(give, 0, 1)
    got, first[-1], tok_x = lax.optimization_barrier((got, first[-1], tok_x))
    first = jnp.concatenate(first)
    joined = keep + got.astype(F32)
    sums = joined[0]
    for k in [2, 1, *range(3, pairs)]:
        sums = sums + swap(joined[k].astype(BF16), 0, chip(k)).astype(F32)
    second = swap(first, 0, chip(1))
    far_first = swap(first, 0, 1)
    channels = particles.shape[1]
    counts = jnp.sum(sums[:, 2 * channels :], axis=1, keepdims=True)
    pooled = jnp.concatenate(
        [sums[:, :channels] / jnp.maximum(counts, 1.0), sums[:, channels : 2 * channels]], axis=1
    ).astype(BF16)
    pooled = [pooled] + [swap(pooled, k, odd(k)) for k in range(1, parts)]
    second, pooled = lax.optimization_barrier((second, pooled))
    far_second = swap(second, 0, 1)
    tok = [tok[0], tok_x[0]] + [tok[k] for k in range(2, parts)]
    hid, query = hidden(tok, pooled, first, far_first, w_in)
    up, keep, give = attend(pooled, hid, query, second, far_second, w_out)

    joined = keep.astype(F32) + swap(give, 0, 1).astype(F32)
    unpooled = up[0].astype(F32)
    for k in range(1, parts):
        unpooled = unpooled + swap(up[k], k, odd(k)).astype(F32)
    near = unpooled.astype(BF16)[None]
    for k in [1 << i for i in range(pairs.bit_length() - 1)]:
        near = jnp.concatenate([near, swap(near, 0, chip(k))])
    far = swap(near, 0, 1)
    particle_out = unpool(particles, clusters, owners, near, far)

    grad = joined[0]
    for k in [pairs - 1, *range(1, pairs - 1)]:
        grad = grad + swap(joined[k].astype(BF16), 0, chip(k)).astype(F32)
    if n_group > parts:
        part_sum = grad.astype(BF16)
        for k in range(1, n_group // parts):
            grad = grad + swap(part_sum, k * parts, 0).astype(F32)
    grad = grad.astype(BF16)
    qk_grad = spread([swap(grad, k, 1) for k in range(parts)])
    return (particle_out, qk_grad)


def solution(mesh):
    placed = (
        P(("group", "shard"), None),
        P("shard", None),
        P(),
        P(),
        P(("group", "shard"), None),
        P(("group", "shard"), None),
        P(("group", "shard")),
        P(("group", "shard")),
    )
    return jax.shard_map(
        local,
        mesh=mesh,
        in_specs=placed,
        out_specs=(P(("group", "shard"), None), P("shard", None)),
        check_vma=False,
    )
```

```python
import functools
import math

import jax
import jax.numpy as jnp
from jax import lax
from jax.experimental import pallas as pl
from jax.experimental.pallas import tpu as pltpu
from jax.sharding import PartitionSpec as P

HEADS = 8
F32 = jnp.float32
BF16 = jnp.bfloat16
VMEM = pl.BlockSpec(memory_space=pltpu.VMEM)


def params(mib):
    return pltpu.CompilerParams(vmem_limit_bytes=mib << 20)


def contract(a, b, da, db):
    return lax.dot_general(a, b, (((da,), (db,)), ((), ())), preferred_element_type=F32)


def pool_kernel(
    owners_hbm, clusters_hbm, feat_hbm, grad_hbm, keep_ref, give_ref, acc_ref, rows_ref, sems, owners_ref, clusters_ref
):
    blocks, rows = clusters_ref.shape
    pairs, t_rows, _ = keep_ref.shape
    width = feat_hbm.shape[1]
    copies = [
        pltpu.make_async_copy(owners_hbm, owners_ref, sems.at[0]),
        pltpu.make_async_copy(clusters_hbm, clusters_ref, sems.at[1]),
        pltpu.make_async_copy(feat_hbm, rows_ref.at[0], sems.at[2]),
        pltpu.make_async_copy(grad_hbm, rows_ref.at[1], sems.at[3]),
    ]
    for copy in copies:
        copy.start()
    acc_ref[...] = jnp.zeros_like(acc_ref)
    for copy in copies:
        copy.wait()
    token = lax.broadcasted_iota(jnp.int32, (t_rows, rows), 0)
    for b in range(blocks):
        member = (clusters_ref[b : b + 1, :] == token).astype(F32)
        span = pl.ds(b * rows, rows)
        both = jnp.concatenate([rows_ref[0, span, :], rows_ref[1, span, :]], axis=1)
        sums = jnp.dot(member.astype(BF16), both, preferred_element_type=F32)
        place = pl.ds(pl.multiple_of(owners_ref[b] * t_rows, t_rows), t_rows)
        acc_ref[place, : 2 * width] += sums
        acc_ref[place, 2 * width :] += member
    me = lax.axis_index("shard")
    for k in range(pairs):
        mine = me ^ chip(k)
        keep_ref[k] = acc_ref[pl.ds(pl.multiple_of(mine * t_rows, t_rows), t_rows), :]
        other = mine ^ 1
        give_ref[k] = acc_ref[pl.ds(pl.multiple_of(other * t_rows, t_rows), t_rows), :].astype(BF16)


def pool(particles, cotangent, clusters, owners, t_rows, n_shard):
    num_blocks = owners.shape[0]
    count, width = particles.shape
    rows = count // num_blocks
    shape = (n_shard // 2, t_rows, 2 * width + rows)
    whole = pl.BlockSpec(memory_space=pl.ANY)
    return pl.pallas_call(
        pool_kernel,
        in_specs=[whole] * 4,
        out_specs=[VMEM, VMEM],
        out_shape=[jax.ShapeDtypeStruct(shape, F32), jax.ShapeDtypeStruct(shape, BF16)],
        scratch_shapes=[
            pltpu.VMEM((n_shard * t_rows, shape[2]), F32),
            pltpu.VMEM((2, count, width), BF16),
            pltpu.SemaphoreType.DMA((4,)),
            pltpu.SMEM(owners.shape, jnp.int32),
            pltpu.VMEM((num_blocks, rows), jnp.int32),
        ],
        compiler_params=params(60),
        cost_estimate=pl.CostEstimate(flops=0, bytes_accessed=3000000, transcendentals=0),
        name="pool",
    )(owners, clusters.reshape(num_blocks, rows), particles, cotangent)


def query_part(hid, near, far, pairs, begin, weight):
    me = lax.axis_index("shard")
    count, rows, _ = near.shape
    total = None
    for i in range(count):
        mine = me ^ chip(reverse(begin + i, pairs))
        core = lax.rem(mine, 2)
        weight[i, pl.ds(pl.multiple_of(core * rows, rows), rows), :] = near[i]
        weight[i, pl.ds(pl.multiple_of((1 - core) * rows, rows), rows), :] = far[i]
        chunk = pl.ds(pl.multiple_of(lax.div(mine, 2) * (2 * rows), 2 * rows), 2 * rows)
        term = jnp.dot(hid[:, chunk], weight[i], preferred_element_type=F32)
        total = term if total is None else total + term
    return total


def hidden_kernel(parts, *refs):
    tok, pooled_refs = refs[:parts], refs[parts : 2 * parts]
    near, far, w_in, hid, query, weight = refs[2 * parts :]
    t_rows, width = tok[0].shape
    channels = w_in.shape[0]
    pooled = jnp.concatenate([r[:, :channels] for r in pooled_refs], axis=0)
    step = 512
    for n in range(0, width, step):
        wide = jnp.dot(pooled, w_in[:, n : n + step], preferred_element_type=F32)
        for k in range(parts):
            span = slice(k * t_rows, (k + 1) * t_rows)
            hid[span, n : n + step] = (
                tok[k][:, n : n + step].astype(F32) + wide[span]
            ).astype(BF16)
    query[...] = query_part(hid, near, far, 2 * near.shape[0], 0, weight)


def hidden(tok, pooled, near, far, w_in):
    parts = len(tok)
    t_rows, width = tok[0].shape
    half, rows, cols = near.shape
    return pl.pallas_call(
        functools.partial(hidden_kernel, parts),
        in_specs=[VMEM] * (2 * parts + 3),
        out_specs=[VMEM] * 2,
        out_shape=[
            jax.ShapeDtypeStruct((parts * t_rows, width), BF16),
            jax.ShapeDtypeStruct((parts * t_rows, cols), F32),
        ],
        scratch_shapes=[pltpu.VMEM((half, 2 * rows, cols), BF16)],
        compiler_params=params(20),
        name="hidden",
    )(*tok, *pooled, near, far, w_in)


def attend_kernel(parts, *refs):
    pooled_refs = refs[:parts]
    hid, query, near, far, w_out, up_ref, keep_ref, give_ref, weight, term = refs[parts:]
    half_pairs, rows, cols = near.shape
    pairs = 2 * half_pairs
    total, width = hid.shape
    t_rows = total // parts
    head_cols = cols * parts
    channels = w_out.shape[1]
    group, me = lax.axis_index("group"), lax.axis_index("shard")
    part = lax.rem(group, parts)
    core = lax.rem(me, 2)
    pair = lax.div(me, 2)
    queries = (query[...] + query_part(hid, near, far, pairs, half_pairs, weight)).astype(BF16)
    pooled_grad = jnp.concatenate([r[:, channels:] for r in pooled_refs], axis=0)
    first = pl.ds(pl.multiple_of(part * cols, cols), cols)
    values = hid[:, first]
    out_w = w_out[first, :]
    out_grad = contract(pooled_grad, out_w, 1, 1).astype(BF16)
    dim = head_cols // HEADS
    scale = 1.0 / math.sqrt(dim)
    row = lax.broadcasted_iota(jnp.int32, (total, total), 0)
    col = lax.broadcasted_iota(jnp.int32, (total, total), 1)
    same = lax.div(row, t_rows) == lax.div(col, t_rows)
    outs, grads = [], []
    for h in range(cols // dim):
        lanes = slice(h * dim, (h + 1) * dim)
        q, v, g = queries[:, lanes], values[:, lanes], out_grad[:, lanes]
        scores = contract(q, q, 1, 1) * scale
        scores = jnp.where(row == col, -1000000000.0, scores)
        scores = jnp.where(same, scores, -3.0e38)
        e = jnp.exp(scores - jnp.max(scores, axis=1, keepdims=True))
        prob = e / jnp.sum(e, axis=1, keepdims=True)
        attended = jnp.dot(prob.astype(BF16), v, preferred_element_type=F32)
        outs.append((v.astype(F32) + attended).astype(BF16))
        prob_grad = contract(g, v, 1, 1)
        inner = jnp.sum(prob_grad * prob, axis=1, keepdims=True)
        score_grad = (prob * (prob_grad - inner) * scale).astype(BF16)
        grads.append(
            jnp.dot(score_grad, q, preferred_element_type=F32) + contract(score_grad, q, 0, 0)
        )
    output = jnp.concatenate(outs, axis=1)
    q_grad = jnp.concatenate(grads, axis=1).astype(BF16)
    rest = (width - head_cols) // parts
    second = pl.ds(pl.multiple_of(head_cols + part * rest, rest), rest)
    up = jnp.dot(output, out_w, preferred_element_type=F32) + jnp.dot(
        hid[:, second], w_out[second, :], preferred_element_type=F32
    )
    for k in range(parts):
        up_ref[k] = up[k * t_rows : (k + 1) * t_rows].astype(BF16)
    for k in range(pairs):
        chunk = pl.ds(pl.multiple_of((pair ^ k) * (2 * rows), 2 * rows), 2 * rows)
        term[...] = contract(hid[:, chunk], q_grad, 0, 0)
        mine = 1 ^ core ^ odd(k)
        keep_ref[k] = term[pl.ds(pl.multiple_of(mine * rows, rows), rows), :].astype(BF16)
        give_ref[k] = term[pl.ds(pl.multiple_of((1 - mine) * rows, rows), rows), :].astype(BF16)


def attend(pooled, hid, query, near, far, w_out):
    parts = len(pooled)
    half, rows, cols = near.shape
    channels = w_out.shape[1]
    t_rows = pooled[0].shape[0]
    shape = jax.ShapeDtypeStruct((2 * half, rows, cols), BF16)
    return pl.pallas_call(
        functools.partial(attend_kernel, parts),
        in_specs=[VMEM] * (parts + 5),
        out_specs=[VMEM] * 3,
        out_shape=[jax.ShapeDtypeStruct((parts, t_rows, channels), BF16), shape, shape],
        scratch_shapes=[
            pltpu.VMEM((half, 2 * rows, cols), BF16),
            pltpu.VMEM((2 * rows, cols), F32),
        ],
        compiler_params=params(20),
        cost_estimate=pl.CostEstimate(flops=0, bytes_accessed=3000000, transcendentals=0),
        name="attend",
    )(*pooled, hid, query, near, far, w_out)


def unpool_kernel(owners_ref, clusters_ref, feat_ref, near, far, out_ref, rows_ref):
    step = pl.program_id(0)
    blocks, rows = clusters_ref.shape
    pairs, t_rows, _ = near.shape

    @pl.when(step == 0)
    def _():
        me = lax.axis_index("shard")
        for k in range(pairs):
            mine = me ^ chip(k)
            rows_ref[pl.ds(pl.multiple_of(mine * t_rows, t_rows), t_rows), :] = near[k]
            rows_ref[pl.ds(pl.multiple_of((mine ^ 1) * t_rows, t_rows), t_rows), :] = far[k]

    token = lax.broadcasted_iota(jnp.int32, (t_rows, rows), 0)
    for b in range(blocks):
        member = (clusters_ref[b : b + 1, :] == token).astype(F32).astype(BF16)
        place = pl.ds(pl.multiple_of(owners_ref[step * blocks + b] * t_rows, t_rows), t_rows)
        span = pl.ds(b * rows, rows)
        picked = contract(member, rows_ref[place, :], 0, 0)
        out_ref[span, :] = (feat_ref[span, :].astype(F32) + picked).astype(BF16)


def unpool(particles, clusters, owners, near, far):
    num_blocks = owners.shape[0]
    count, width = particles.shape
    rows = count // num_blocks
    steps = 4
    pairs, t_rows, _ = near.shape
    whole = pl.BlockSpec(near.shape, lambda i, own: (0, 0, 0))
    return pl.pallas_call(
        unpool_kernel,
        grid_spec=pltpu.PrefetchScalarGridSpec(
            num_scalar_prefetch=1,
            grid=(steps,),
            in_specs=[
                pl.BlockSpec((num_blocks // steps, rows), lambda i, own: (i, 0)),
                pl.BlockSpec((count // steps, width), lambda i, own: (i, 0)),
                whole,
                whole,
            ],
            out_specs=pl.BlockSpec((count // steps, width), lambda i, own: (i, 0)),
            scratch_shapes=[pltpu.VMEM((2 * pairs * t_rows, width), BF16)],
        ),
        out_shape=jax.ShapeDtypeStruct(particles.shape, BF16),
        compiler_params=params(16),
        name="unpool",
    )(owners, clusters.reshape(num_blocks, rows), particles, near, far)


def spread_kernel(*refs):
    pieces, out_ref = refs[:-1], refs[-1]
    part = lax.rem(lax.axis_index("group"), len(pieces))
    cols = pieces[0].shape[1]
    for k, piece in enumerate(pieces):
        out_ref[:, pl.ds(pl.multiple_of((part ^ k) * cols, cols), cols)] = piece[...].astype(F32)


def spread(pieces):
    rows, cols = pieces[0].shape
    return pl.pallas_call(
        spread_kernel,
        in_specs=[VMEM] * len(pieces),
        out_specs=VMEM,
        out_shape=jax.ShapeDtypeStruct((rows, cols * len(pieces)), F32),
        compiler_params=params(16),
        name="spread",
    )(*pieces)


def swap(x, group, shard):
    n = lax.axis_size("shard")
    flip = group * n + shard
    pairs = [(i, i ^ flip) for i in range(lax.axis_size("group") * n)]
    return lax.ppermute(x, ("group", "shard"), pairs)


def odd(k):
    return bin(k).count("1") % 2


def reverse(k, count):
    bits = count.bit_length() - 1
    return sum(((k >> i) & 1) << (bits - 1 - i) for i in range(bits))


def chip(k):
    return 2 * k + odd(k)


def local(tokens, w_qk, w_in, w_out, particles, cotangent, clusters, owners):
    n_group, n_shard = lax.axis_size("group"), lax.axis_size("shard")
    parts = math.gcd(n_group, 4)
    pairs = n_shard // 2
    t_rows = tokens.shape[0]
    channels = particles.shape[1]
    cols = w_qk.shape[1] // parts
    part = lax.rem(lax.axis_index("group"), parts)

    w_own = lax.dynamic_slice_in_dim(w_qk, part * cols, cols, axis=1)
    bits = [pairs >> i for i in range(1, pairs.bit_length())]
    first = [w_own[None]]
    for k in bits[:-1]:
        first.append(swap(jnp.concatenate(first), 0, chip(k)))
    tok_x = swap(tokens[None], 1, 1)
    tok = jnp.concatenate([tokens[None], tok_x])
    for k in [1 << i for i in range(1, parts.bit_length() - 1)]:
        tok = jnp.concatenate([tok, swap(tok, k, 1)])

    keep, give = pool(particles, cotangent, clusters, owners, t_rows, n_shard)
    got = swap(give, 0, 1)
    got, first[-1], tok_x = lax.optimization_barrier((got, first[-1], tok_x))
    first = jnp.concatenate(first)
    joined = keep + got.astype(F32)
    got = [swap(joined[k].astype(BF16), 0, chip(k)) for k in [2, 1, *range(3, pairs)]]
    far_first = swap(first, 0, 1)
    second = swap(first, 0, chip(1))
    sums = joined[0]
    for piece in got:
        sums = sums + piece.astype(F32)
    counts = jnp.sum(sums[:, 2 * channels :], axis=1, keepdims=True)
    pooled = jnp.concatenate(
        [sums[:, :channels] / jnp.maximum(counts, 1.0), sums[:, channels : 2 * channels]], axis=1
    ).astype(BF16)
    pooled = [pooled] + [swap(pooled, k, odd(k)) for k in range(1, parts)]
    second, pooled = lax.optimization_barrier((second, pooled))
    far_second = swap(second, 0, 1)
    tok = [tokens, tok_x[0]] + [tok[k] for k in range(2, parts)]
    hid, query = hidden(tok, pooled, first, far_first, w_in)
    up, keep, give = attend(pooled, hid, query, second, far_second, w_out)
    joined = keep.astype(F32) + swap(give, 0, 1).astype(F32)

    unpooled = up[0].astype(F32)
    for k in [*range(2, parts), 1]:
        unpooled = unpooled + swap(up[k], k, odd(k)).astype(F32)
    near = unpooled.astype(BF16)[None]
    for k in [1 << i for i in range(pairs.bit_length() - 1)]:
        near = jnp.concatenate([near, swap(near, 0, chip(k))])
    far = swap(near, 0, 1)
    particle_out = unpool(particles, clusters, owners, near, far)

    grad = joined[0]
    for k in [pairs - 1, *range(1, pairs - 1)]:
        grad = grad + swap(joined[k].astype(BF16), 0, chip(k)).astype(F32)
    grad = grad.astype(BF16)
    if n_group > parts:
        part_sum = grad
        grad = grad.astype(F32)
        for k in range(1, n_group // parts):
            grad = grad + swap(part_sum, k * parts, 0).astype(F32)
        grad = grad.astype(BF16)
    pieces = {k: swap(grad, k, 1) for k in [*range(1, parts), 0]}
    qk_grad = spread([pieces[k] for k in range(parts)])
    return (particle_out, qk_grad)


def solution(mesh):
    placed = (
        P(("group", "shard"), None),
        P("shard", None),
        P(),
        P(),
        P(("group", "shard"), None),
        P(("group", "shard"), None),
        P(("group", "shard")),
        P(("group", "shard")),
    )
    return jax.shard_map(
        local,
        mesh=mesh,
        in_specs=placed,
        out_specs=(P(("group", "shard"), None), P("shard", None)),
        check_vma=False,
    )
```

```python
import functools
import math

import jax
import jax.numpy as jnp
from jax import lax
from jax.experimental import pallas as pl
from jax.experimental.pallas import tpu as pltpu
from jax.sharding import PartitionSpec as P

HEADS = 8
F32 = jnp.float32
BF16 = jnp.bfloat16
VMEM = pl.BlockSpec(memory_space=pltpu.VMEM)


def params(mib):
    return pltpu.CompilerParams(vmem_limit_bytes=mib << 20)


def contract(a, b, da, db):
    return lax.dot_general(a, b, (((da,), (db,)), ((), ())), preferred_element_type=F32)


def pool_kernel(
    owners_hbm, clusters_hbm, feat_hbm, grad_hbm, keep_ref, give_ref, acc_ref, rows_ref, sems, owners_ref, clusters_ref
):
    blocks, rows = clusters_ref.shape
    pairs, t_rows, _ = keep_ref.shape
    width = feat_hbm.shape[1]
    copies = [
        pltpu.make_async_copy(owners_hbm, owners_ref, sems.at[0]),
        pltpu.make_async_copy(clusters_hbm, clusters_ref, sems.at[1]),
        pltpu.make_async_copy(feat_hbm, rows_ref.at[0], sems.at[2]),
        pltpu.make_async_copy(grad_hbm, rows_ref.at[1], sems.at[3]),
    ]
    for copy in copies:
        copy.start()
    acc_ref[...] = jnp.zeros_like(acc_ref)
    for copy in copies:
        copy.wait()
    token = lax.broadcasted_iota(jnp.int32, (t_rows, rows), 0)
    for b in range(blocks):
        member = (clusters_ref[b : b + 1, :] == token).astype(F32)
        span = pl.ds(b * rows, rows)
        both = jnp.concatenate([rows_ref[0, span, :], rows_ref[1, span, :]], axis=1)
        sums = jnp.dot(member.astype(BF16), both, preferred_element_type=F32)
        place = pl.ds(pl.multiple_of(owners_ref[b] * t_rows, t_rows), t_rows)
        acc_ref[place, : 2 * width] += sums
        acc_ref[place, 2 * width :] += member
    me = lax.axis_index("shard")
    for k in range(pairs):
        mine = me ^ chip(k)
        keep_ref[k] = acc_ref[pl.ds(pl.multiple_of(mine * t_rows, t_rows), t_rows), :]
        other = mine ^ 1
        give_ref[k] = acc_ref[pl.ds(pl.multiple_of(other * t_rows, t_rows), t_rows), :].astype(BF16)


def pool(particles, cotangent, clusters, owners, t_rows, n_shard):
    num_blocks = owners.shape[0]
    count, width = particles.shape
    rows = count // num_blocks
    shape = (n_shard // 2, t_rows, 2 * width + rows)
    whole = pl.BlockSpec(memory_space=pl.ANY)
    return pl.pallas_call(
        pool_kernel,
        in_specs=[whole] * 4,
        out_specs=[VMEM, VMEM],
        out_shape=[jax.ShapeDtypeStruct(shape, F32), jax.ShapeDtypeStruct(shape, BF16)],
        scratch_shapes=[
            pltpu.VMEM((n_shard * t_rows, shape[2]), F32),
            pltpu.VMEM((2, count, width), BF16),
            pltpu.SemaphoreType.DMA((4,)),
            pltpu.SMEM(owners.shape, jnp.int32),
            pltpu.VMEM((num_blocks, rows), jnp.int32),
        ],
        compiler_params=params(60),
        cost_estimate=pl.CostEstimate(flops=0, bytes_accessed=3000000, transcendentals=0),
        name="pool",
    )(owners, clusters.reshape(num_blocks, rows), particles, cotangent)


def query_part(hid, near, far, pairs, begin, weight):
    me = lax.axis_index("shard")
    count, rows, _ = near.shape
    total = None
    for i in range(count):
        mine = me ^ chip(reverse(begin + i, pairs))
        if rows % 128 == 0:
            term = 0.0
            for piece, owner in ((near, mine), (far, mine ^ 1)):
                chunk = pl.ds(pl.multiple_of(owner * rows, rows), rows)
                term += jnp.dot(hid[:, chunk], piece[i], preferred_element_type=F32)
        else:
            core = lax.rem(mine, 2)
            weight[i, pl.ds(pl.multiple_of(core * rows, rows), rows), :] = near[i]
            weight[i, pl.ds(pl.multiple_of((1 - core) * rows, rows), rows), :] = far[i]
            chunk = pl.ds(pl.multiple_of(lax.div(mine, 2) * (2 * rows), 2 * rows), 2 * rows)
            term = jnp.dot(hid[:, chunk], weight[i], preferred_element_type=F32)
        total = term if total is None else total + term
    return total


def hidden_kernel(parts, *refs):
    tok, pooled_refs = refs[:parts], refs[parts : 2 * parts]
    near, far, w_in, hid, query, weight = refs[2 * parts :]
    t_rows, width = tok[0].shape
    channels = w_in.shape[0]
    pooled = jnp.concatenate([r[:, :channels] for r in pooled_refs], axis=0)
    step = 512
    for n in range(0, width, step):
        wide = jnp.dot(pooled, w_in[:, n : n + step], preferred_element_type=F32)
        for k in range(parts):
            span = slice(k * t_rows, (k + 1) * t_rows)
            hid[span, n : n + step] = (
                tok[k][:, n : n + step].astype(F32) + wide[span]
            ).astype(BF16)
    query[...] = query_part(hid, near, far, 2 * near.shape[0], 0, weight)


def hidden(tok, pooled, near, far, w_in):
    parts = len(tok)
    t_rows, width = tok[0].shape
    half, rows, cols = near.shape
    return pl.pallas_call(
        functools.partial(hidden_kernel, parts),
        in_specs=[VMEM] * (2 * parts + 3),
        out_specs=[VMEM] * 2,
        out_shape=[
            jax.ShapeDtypeStruct((parts * t_rows, width), BF16),
            jax.ShapeDtypeStruct((parts * t_rows, cols), F32),
        ],
        scratch_shapes=[pltpu.VMEM((half, 2 * rows, cols), BF16)],
        compiler_params=params(20),
        name="hidden",
    )(*tok, *pooled, near, far, w_in)


def attend_kernel(parts, *refs):
    pooled_refs = refs[:parts]
    hid, query, near, far, w_out, up_ref, keep_ref, give_ref, weight, term = refs[parts:]
    half_pairs, rows, cols = near.shape
    pairs = 2 * half_pairs
    total, width = hid.shape
    t_rows = total // parts
    head_cols = cols * parts
    channels = w_out.shape[1]
    group, me = lax.axis_index("group"), lax.axis_index("shard")
    part = lax.rem(group, parts)
    core = lax.rem(me, 2)
    pair = lax.div(me, 2)
    queries = (query[...] + query_part(hid, near, far, pairs, half_pairs, weight)).astype(BF16)
    pooled_grad = jnp.concatenate([r[:, channels:] for r in pooled_refs], axis=0)
    first = pl.ds(pl.multiple_of(part * cols, cols), cols)
    values = hid[:, first]
    out_w = w_out[first, :]
    out_grad = contract(pooled_grad, out_w, 1, 1).astype(BF16)
    dim = head_cols // HEADS
    scale = 1.0 / math.sqrt(dim)
    row = lax.broadcasted_iota(jnp.int32, (total, total), 0)
    col = lax.broadcasted_iota(jnp.int32, (total, total), 1)
    same = lax.div(row, t_rows) == lax.div(col, t_rows)
    outs, grads = [], []
    for h in range(cols // dim):
        lanes = slice(h * dim, (h + 1) * dim)
        q, v, g = queries[:, lanes], values[:, lanes], out_grad[:, lanes]
        scores = contract(q, q, 1, 1) * scale
        scores = jnp.where(row == col, -1000000000.0, scores)
        scores = jnp.where(same, scores, -3.0e38)
        e = jnp.exp(scores - jnp.max(scores, axis=1, keepdims=True))
        prob = e / jnp.sum(e, axis=1, keepdims=True)
        attended = jnp.dot(prob.astype(BF16), v, preferred_element_type=F32)
        outs.append((v.astype(F32) + attended).astype(BF16))
        prob_grad = contract(g, v, 1, 1)
        inner = jnp.sum(prob_grad * prob, axis=1, keepdims=True)
        score_grad = (prob * (prob_grad - inner) * scale).astype(BF16)
        grads.append(
            jnp.dot(score_grad, q, preferred_element_type=F32) + contract(score_grad, q, 0, 0)
        )
    output = jnp.concatenate(outs, axis=1)
    q_grad = jnp.concatenate(grads, axis=1).astype(BF16)
    rest = (width - head_cols) // parts
    second = pl.ds(pl.multiple_of(head_cols + part * rest, rest), rest)
    up = jnp.dot(output, out_w, preferred_element_type=F32) + jnp.dot(
        hid[:, second], w_out[second, :], preferred_element_type=F32
    )
    for k in range(parts):
        up_ref[k] = up[k * t_rows : (k + 1) * t_rows].astype(BF16)
    for k in range(pairs):
        mine = 1 ^ core ^ odd(k)
        if rows % 128 == 0:
            for out_ref, owner in ((keep_ref, mine), (give_ref, 1 - mine)):
                chunk = pl.ds(pl.multiple_of((pair ^ k) * (2 * rows) + owner * rows, rows), rows)
                out_ref[k] = contract(hid[:, chunk], q_grad, 0, 0).astype(BF16)
        else:
            chunk = pl.ds(pl.multiple_of((pair ^ k) * (2 * rows), 2 * rows), 2 * rows)
            term[...] = contract(hid[:, chunk], q_grad, 0, 0)
            keep_ref[k] = term[pl.ds(pl.multiple_of(mine * rows, rows), rows), :].astype(BF16)
            give_ref[k] = term[pl.ds(pl.multiple_of((1 - mine) * rows, rows), rows), :].astype(BF16)


def attend(pooled, hid, query, near, far, w_out):
    parts = len(pooled)
    half, rows, cols = near.shape
    channels = w_out.shape[1]
    t_rows = pooled[0].shape[0]
    shape = jax.ShapeDtypeStruct((2 * half, rows, cols), BF16)
    return pl.pallas_call(
        functools.partial(attend_kernel, parts),
        in_specs=[VMEM] * (parts + 5),
        out_specs=[VMEM] * 3,
        out_shape=[jax.ShapeDtypeStruct((parts, t_rows, channels), BF16), shape, shape],
        scratch_shapes=[
            pltpu.VMEM((half, 2 * rows, cols), BF16),
            pltpu.VMEM((2 * rows, cols), F32),
        ],
        compiler_params=params(20),
        cost_estimate=pl.CostEstimate(flops=0, bytes_accessed=3000000, transcendentals=0),
        name="attend",
    )(*pooled, hid, query, near, far, w_out)


def unpool_kernel(owners_ref, clusters_ref, feat_ref, near, far, out_ref, rows_ref):
    step = pl.program_id(0)
    blocks, rows = clusters_ref.shape
    pairs, t_rows, _ = near.shape

    @pl.when(step == 0)
    def _():
        me = lax.axis_index("shard")
        for k in range(pairs):
            mine = me ^ chip(k)
            rows_ref[pl.ds(pl.multiple_of(mine * t_rows, t_rows), t_rows), :] = near[k]
            rows_ref[pl.ds(pl.multiple_of((mine ^ 1) * t_rows, t_rows), t_rows), :] = far[k]

    token = lax.broadcasted_iota(jnp.int32, (t_rows, rows), 0)
    for b in range(blocks):
        member = (clusters_ref[b : b + 1, :] == token).astype(F32).astype(BF16)
        place = pl.ds(pl.multiple_of(owners_ref[step * blocks + b] * t_rows, t_rows), t_rows)
        span = pl.ds(b * rows, rows)
        picked = contract(member, rows_ref[place, :], 0, 0)
        out_ref[span, :] = (feat_ref[span, :].astype(F32) + picked).astype(BF16)


def unpool(particles, clusters, owners, near, far):
    num_blocks = owners.shape[0]
    count, width = particles.shape
    rows = count // num_blocks
    steps = 4
    pairs, t_rows, _ = near.shape
    whole = pl.BlockSpec(near.shape, lambda i, own: (0, 0, 0))
    return pl.pallas_call(
        unpool_kernel,
        grid_spec=pltpu.PrefetchScalarGridSpec(
            num_scalar_prefetch=1,
            grid=(steps,),
            in_specs=[
                pl.BlockSpec((num_blocks // steps, rows), lambda i, own: (i, 0)),
                pl.BlockSpec((count // steps, width), lambda i, own: (i, 0)),
                whole,
                whole,
            ],
            out_specs=pl.BlockSpec((count // steps, width), lambda i, own: (i, 0)),
            scratch_shapes=[pltpu.VMEM((2 * pairs * t_rows, width), BF16)],
        ),
        out_shape=jax.ShapeDtypeStruct(particles.shape, BF16),
        compiler_params=params(16),
        name="unpool",
    )(owners, clusters.reshape(num_blocks, rows), particles, near, far)


def spread_kernel(*refs):
    pieces, out_ref = refs[:-1], refs[-1]
    part = lax.rem(lax.axis_index("group"), len(pieces))
    cols = pieces[0].shape[1]
    for k, piece in enumerate(pieces):
        out_ref[:, pl.ds(pl.multiple_of((part ^ k) * cols, cols), cols)] = piece[...].astype(F32)


def spread(pieces):
    rows, cols = pieces[0].shape
    return pl.pallas_call(
        spread_kernel,
        in_specs=[VMEM] * len(pieces),
        out_specs=VMEM,
        out_shape=jax.ShapeDtypeStruct((rows, cols * len(pieces)), F32),
        compiler_params=params(16),
        name="spread",
    )(*pieces)


def swap(x, group, shard):
    n = lax.axis_size("shard")
    flip = group * n + shard
    pairs = [(i, i ^ flip) for i in range(lax.axis_size("group") * n)]
    return lax.ppermute(x, ("group", "shard"), pairs)


def odd(k):
    return bin(k).count("1") % 2


def reverse(k, count):
    bits = count.bit_length() - 1
    return sum(((k >> i) & 1) << (bits - 1 - i) for i in range(bits))


def chip(k):
    return 2 * k + odd(k)


def local(tokens, w_qk, w_in, w_out, particles, cotangent, clusters, owners):
    n_group, n_shard = lax.axis_size("group"), lax.axis_size("shard")
    parts = math.gcd(n_group, 4)
    pairs = n_shard // 2
    t_rows = tokens.shape[0]
    channels = particles.shape[1]
    cols = w_qk.shape[1] // parts
    part = lax.rem(lax.axis_index("group"), parts)

    w_own = lax.dynamic_slice_in_dim(w_qk, part * cols, cols, axis=1)
    bits = [pairs >> i for i in range(1, pairs.bit_length())]
    first = [w_own[None]]
    for k in bits[:-1]:
        first.append(swap(jnp.concatenate(first), 0, chip(k)))
    tok_x = swap(tokens[None], 1, 1)
    tok = jnp.concatenate([tokens[None], tok_x])
    for k in [1 << i for i in range(1, parts.bit_length() - 1)]:
        tok = jnp.concatenate([tok, swap(tok, k, 1)])

    keep, give = pool(particles, cotangent, clusters, owners, t_rows, n_shard)
    got = swap(give, 0, 1)
    got, first[-1], tok_x = lax.optimization_barrier((got, first[-1], tok_x))
    first = jnp.concatenate(first)
    joined = keep + got.astype(F32)
    got = [swap(joined[k].astype(BF16), 0, chip(k)) for k in [2, 1, *range(3, pairs)]]
    far_first = swap(first, 0, 1)
    second = swap(first, 0, chip(1))
    sums = joined[0]
    for piece in got:
        sums = sums + piece.astype(F32)
    counts = jnp.sum(sums[:, 2 * channels :], axis=1, keepdims=True)
    pooled = jnp.concatenate(
        [sums[:, :channels] / jnp.maximum(counts, 1.0), sums[:, channels : 2 * channels]], axis=1
    ).astype(BF16)
    pooled = [pooled] + [swap(pooled, k, odd(k)) for k in range(1, parts)]
    second, pooled = lax.optimization_barrier((second, pooled))
    far_second = swap(second, 0, 1)
    tok = [tokens, tok_x[0]] + [tok[k] for k in range(2, parts)]
    hid, query = hidden(tok, pooled, first, far_first, w_in)
    up, keep, give = attend(pooled, hid, query, second, far_second, w_out)
    joined = keep.astype(F32) + swap(give, 0, 1).astype(F32)

    unpooled = up[0].astype(F32)
    for k in [*range(2, parts), 1]:
        unpooled = unpooled + swap(up[k], k, odd(k)).astype(F32)
    near = unpooled.astype(BF16)[None]
    for k in [1 << i for i in range(pairs.bit_length() - 1)]:
        near = jnp.concatenate([near, swap(near, 0, chip(k))])
    far = swap(near, 0, 1)
    particle_out = unpool(particles, clusters, owners, near, far)

    grad = joined[0]
    for k in [pairs - 1, *range(1, pairs - 1)]:
        grad = grad + swap(joined[k].astype(BF16), 0, chip(k)).astype(F32)
    grad = grad.astype(BF16)
    if n_group > parts:
        part_sum = grad
        grad = grad.astype(F32)
        for k in range(1, n_group // parts):
            grad = grad + swap(part_sum, k * parts, 0).astype(F32)
        grad = grad.astype(BF16)
    pieces = {k: swap(grad, k, 1) for k in [*range(1, parts), 0]}
    qk_grad = spread([pieces[k] for k in range(parts)])
    return (particle_out, qk_grad)


def solution(mesh):
    placed = (
        P(("group", "shard"), None),
        P("shard", None),
        P(),
        P(),
        P(("group", "shard"), None),
        P(("group", "shard"), None),
        P(("group", "shard")),
        P(("group", "shard")),
    )
    return jax.shard_map(
        local,
        mesh=mesh,
        in_specs=placed,
        out_specs=(P(("group", "shard"), None), P("shard", None)),
        check_vma=False,
    )
```

```python
import functools
import math

import jax
import jax.numpy as jnp
from jax import lax
from jax.experimental import pallas as pl
from jax.experimental.pallas import tpu as pltpu
from jax.sharding import PartitionSpec as P

HEADS = 8
F32 = jnp.float32
BF16 = jnp.bfloat16
VMEM = pl.BlockSpec(memory_space=pltpu.VMEM)


def params(mib):
    return pltpu.CompilerParams(vmem_limit_bytes=mib << 20)


def contract(a, b, da, db):
    return lax.dot_general(a, b, (((da,), (db,)), ((), ())), preferred_element_type=F32)


def pool_kernel(
    owners_hbm, clusters_hbm, feat_hbm, grad_hbm, keep_ref, give_ref, acc_ref, rows_ref, sems, owners_ref, clusters_ref
):
    blocks, rows = clusters_ref.shape
    pairs, t_rows, _ = keep_ref.shape
    width = feat_hbm.shape[1]
    copies = [
        pltpu.make_async_copy(owners_hbm, owners_ref, sems.at[0]),
        pltpu.make_async_copy(clusters_hbm, clusters_ref, sems.at[1]),
        pltpu.make_async_copy(feat_hbm, rows_ref.at[0], sems.at[2]),
        pltpu.make_async_copy(grad_hbm, rows_ref.at[1], sems.at[3]),
    ]
    for copy in copies:
        copy.start()
    acc_ref[...] = jnp.zeros_like(acc_ref)
    for copy in copies:
        copy.wait()
    token = lax.broadcasted_iota(jnp.int32, (t_rows, rows), 0)
    for b in range(blocks):
        member = (clusters_ref[b : b + 1, :] == token).astype(F32)
        span = pl.ds(b * rows, rows)
        both = jnp.concatenate([rows_ref[0, span, :], rows_ref[1, span, :]], axis=1)
        sums = jnp.dot(member.astype(BF16), both, preferred_element_type=F32)
        place = pl.ds(pl.multiple_of(owners_ref[b] * t_rows, t_rows), t_rows)
        acc_ref[place, : 2 * width] += sums
        acc_ref[place, 2 * width :] += member
    me = lax.axis_index("shard")
    for k in range(pairs):
        mine = me ^ chip(k)
        keep_ref[k] = acc_ref[pl.ds(pl.multiple_of(mine * t_rows, t_rows), t_rows), :]
        other = mine ^ 1
        give_ref[k] = acc_ref[pl.ds(pl.multiple_of(other * t_rows, t_rows), t_rows), :].astype(BF16)


def pool(particles, cotangent, clusters, owners, t_rows, n_shard):
    num_blocks = owners.shape[0]
    count, width = particles.shape
    rows = count // num_blocks
    shape = (n_shard // 2, t_rows, 2 * width + rows)
    whole = pl.BlockSpec(memory_space=pl.ANY)
    return pl.pallas_call(
        pool_kernel,
        in_specs=[whole] * 4,
        out_specs=[VMEM, VMEM],
        out_shape=[jax.ShapeDtypeStruct(shape, F32), jax.ShapeDtypeStruct(shape, BF16)],
        scratch_shapes=[
            pltpu.VMEM((n_shard * t_rows, shape[2]), F32),
            pltpu.VMEM((2, count, width), BF16),
            pltpu.SemaphoreType.DMA((4,)),
            pltpu.SMEM(owners.shape, jnp.int32),
            pltpu.VMEM((num_blocks, rows), jnp.int32),
        ],
        compiler_params=params(60),
        cost_estimate=pl.CostEstimate(flops=0, bytes_accessed=3000000, transcendentals=0),
        name="pool",
    )(owners, clusters.reshape(num_blocks, rows), particles, cotangent)


def query_part(hid, near, far, pairs, begin, weight):
    me = lax.axis_index("shard")
    count, rows, _ = near.shape
    total = None
    for i in range(count):
        mine = me ^ chip(reverse(begin + i, pairs))
        if rows % 128 == 0:
            term = 0.0
            for piece, owner in ((near, mine), (far, mine ^ 1)):
                chunk = pl.ds(pl.multiple_of(owner * rows, rows), rows)
                term += jnp.dot(hid[:, chunk], piece[i], preferred_element_type=F32)
        else:
            core = lax.rem(mine, 2)
            weight[i, pl.ds(pl.multiple_of(core * rows, rows), rows), :] = near[i]
            weight[i, pl.ds(pl.multiple_of((1 - core) * rows, rows), rows), :] = far[i]
            chunk = pl.ds(pl.multiple_of(lax.div(mine, 2) * (2 * rows), 2 * rows), 2 * rows)
            term = jnp.dot(hid[:, chunk], weight[i], preferred_element_type=F32)
        total = term if total is None else total + term
    return total


def hidden_kernel(parts, *refs):
    tok, pooled_refs = refs[:parts], refs[parts : 2 * parts]
    near, far, w_in, hid, query, weight = refs[2 * parts :]
    t_rows, width = tok[0].shape
    channels = w_in.shape[0]
    pooled = jnp.concatenate([r[:, :channels] for r in pooled_refs], axis=0)
    step = 512
    for n in range(0, width, step):
        wide = jnp.dot(pooled, w_in[:, n : n + step], preferred_element_type=F32)
        for k in range(parts):
            span = slice(k * t_rows, (k + 1) * t_rows)
            hid[span, n : n + step] = (
                tok[k][:, n : n + step].astype(F32) + wide[span]
            ).astype(BF16)
    query[...] = query_part(hid, near, far, 2 * near.shape[0], 0, weight)


def hidden(tok, pooled, near, far, w_in):
    parts = len(tok)
    t_rows, width = tok[0].shape
    half, rows, cols = near.shape
    return pl.pallas_call(
        functools.partial(hidden_kernel, parts),
        in_specs=[VMEM] * (2 * parts + 3),
        out_specs=[VMEM] * 2,
        out_shape=[
            jax.ShapeDtypeStruct((parts * t_rows, width), BF16),
            jax.ShapeDtypeStruct((parts * t_rows, cols), F32),
        ],
        scratch_shapes=[pltpu.VMEM((half, 2 * rows, cols), BF16)],
        compiler_params=params(20),
        name="hidden",
    )(*tok, *pooled, near, far, w_in)


def attend_kernel(parts, *refs):
    pooled_refs = refs[:parts]
    hid, query, near, far, w_out, up_ref, keep_ref, give_ref, weight, term = refs[parts:]
    half_pairs, rows, cols = near.shape
    pairs = 2 * half_pairs
    total, width = hid.shape
    t_rows = total // parts
    head_cols = cols * parts
    channels = w_out.shape[1]
    group, me = lax.axis_index("group"), lax.axis_index("shard")
    part = lax.rem(group, parts)
    core = lax.rem(me, 2)
    pair = lax.div(me, 2)
    queries = (query[...] + query_part(hid, near, far, pairs, half_pairs, weight)).astype(BF16)
    pooled_grad = jnp.concatenate([r[:, channels:] for r in pooled_refs], axis=0)
    first = pl.ds(pl.multiple_of(part * cols, cols), cols)
    values = hid[:, first]
    out_w = w_out[first, :]
    out_grad = contract(pooled_grad, out_w, 1, 1).astype(BF16)
    dim = head_cols // HEADS
    scale = 1.0 / math.sqrt(dim)
    row = lax.broadcasted_iota(jnp.int32, (total, total), 0)
    col = lax.broadcasted_iota(jnp.int32, (total, total), 1)
    same = lax.div(row, t_rows) == lax.div(col, t_rows)
    outs, grads = [], []
    for h in range(cols // dim):
        lanes = slice(h * dim, (h + 1) * dim)
        q, v, g = queries[:, lanes], values[:, lanes], out_grad[:, lanes]
        scores = contract(q, q, 1, 1) * scale
        scores = jnp.where(row == col, -1000000000.0, scores)
        scores = jnp.where(same, scores, -3.0e38)
        e = jnp.exp(scores - jnp.max(scores, axis=1, keepdims=True))
        prob = e / jnp.sum(e, axis=1, keepdims=True)
        attended = jnp.dot(prob.astype(BF16), v, preferred_element_type=F32)
        outs.append((v.astype(F32) + attended).astype(BF16))
        prob_grad = contract(g, v, 1, 1)
        inner = jnp.sum(prob_grad * prob, axis=1, keepdims=True)
        score_grad = (prob * (prob_grad - inner) * scale).astype(BF16)
        grads.append(
            jnp.dot(score_grad, q, preferred_element_type=F32) + contract(score_grad, q, 0, 0)
        )
    output = jnp.concatenate(outs, axis=1)
    q_grad = jnp.concatenate(grads, axis=1).astype(BF16)
    rest = (width - head_cols) // parts
    second = pl.ds(pl.multiple_of(head_cols + part * rest, rest), rest)
    up = jnp.dot(output, out_w, preferred_element_type=F32) + jnp.dot(
        hid[:, second], w_out[second, :], preferred_element_type=F32
    )
    for k in range(parts):
        up_ref[k] = up[k * t_rows : (k + 1) * t_rows].astype(BF16)
    for k in range(pairs):
        mine = 1 ^ core ^ odd(k)
        if rows % 128 == 0:
            for out_ref, owner in ((keep_ref, mine), (give_ref, 1 - mine)):
                chunk = pl.ds(pl.multiple_of((pair ^ k) * (2 * rows) + owner * rows, rows), rows)
                out_ref[k] = contract(hid[:, chunk], q_grad, 0, 0).astype(BF16)
        else:
            chunk = pl.ds(pl.multiple_of((pair ^ k) * (2 * rows), 2 * rows), 2 * rows)
            term[...] = contract(hid[:, chunk], q_grad, 0, 0)
            keep_ref[k] = term[pl.ds(pl.multiple_of(mine * rows, rows), rows), :].astype(BF16)
            give_ref[k] = term[pl.ds(pl.multiple_of((1 - mine) * rows, rows), rows), :].astype(BF16)


def attend(pooled, hid, query, near, far, w_out):
    parts = len(pooled)
    half, rows, cols = near.shape
    channels = w_out.shape[1]
    t_rows = pooled[0].shape[0]
    shape = jax.ShapeDtypeStruct((2 * half, rows, cols), BF16)
    return pl.pallas_call(
        functools.partial(attend_kernel, parts),
        in_specs=[VMEM] * (parts + 5),
        out_specs=[VMEM] * 3,
        out_shape=[jax.ShapeDtypeStruct((parts, t_rows, channels), BF16), shape, shape],
        scratch_shapes=[
            pltpu.VMEM((half, 2 * rows, cols), BF16),
            pltpu.VMEM((2 * rows, cols), F32),
        ],
        compiler_params=params(20),
        cost_estimate=pl.CostEstimate(flops=0, bytes_accessed=3000000, transcendentals=0),
        name="attend",
    )(*pooled, hid, query, near, far, w_out)


def unpool_kernel(owners_ref, clusters_ref, feat_ref, near, far, out_ref, rows_ref):
    step = pl.program_id(0)
    blocks, rows = clusters_ref.shape
    pairs, t_rows, _ = near.shape

    @pl.when(step == 0)
    def _():
        me = lax.axis_index("shard")
        for k in range(pairs):
            mine = me ^ chip(k)
            rows_ref[pl.ds(pl.multiple_of(mine * t_rows, t_rows), t_rows), :] = near[k]
            rows_ref[pl.ds(pl.multiple_of((mine ^ 1) * t_rows, t_rows), t_rows), :] = far[k]

    token = lax.broadcasted_iota(jnp.int32, (t_rows, rows), 0)
    for b in range(blocks):
        member = (clusters_ref[b : b + 1, :] == token).astype(F32).astype(BF16)
        place = pl.ds(pl.multiple_of(owners_ref[step * blocks + b] * t_rows, t_rows), t_rows)
        span = pl.ds(b * rows, rows)
        picked = contract(member, rows_ref[place, :], 0, 0)
        out_ref[span, :] = (feat_ref[span, :].astype(F32) + picked).astype(BF16)


def unpool(particles, clusters, owners, near, far):
    num_blocks = owners.shape[0]
    count, width = particles.shape
    rows = count // num_blocks
    steps = 4
    pairs, t_rows, _ = near.shape
    whole = pl.BlockSpec(near.shape, lambda i, own: (0, 0, 0))
    return pl.pallas_call(
        unpool_kernel,
        grid_spec=pltpu.PrefetchScalarGridSpec(
            num_scalar_prefetch=1,
            grid=(steps,),
            in_specs=[
                pl.BlockSpec((num_blocks // steps, rows), lambda i, own: (i, 0)),
                pl.BlockSpec((count // steps, width), lambda i, own: (i, 0)),
                whole,
                whole,
            ],
            out_specs=pl.BlockSpec((count // steps, width), lambda i, own: (i, 0)),
            scratch_shapes=[pltpu.VMEM((2 * pairs * t_rows, width), BF16)],
        ),
        out_shape=jax.ShapeDtypeStruct(particles.shape, BF16),
        compiler_params=params(16),
        name="unpool",
    )(owners, clusters.reshape(num_blocks, rows), particles, near, far)


def spread_kernel(*refs):
    pieces, out_ref = refs[:-1], refs[-1]
    part = lax.rem(lax.axis_index("group"), len(pieces))
    cols = pieces[0].shape[1]
    for k, piece in enumerate(pieces):
        out_ref[:, pl.ds(pl.multiple_of((part ^ k) * cols, cols), cols)] = piece[...].astype(F32)


def spread(pieces):
    rows, cols = pieces[0].shape
    return pl.pallas_call(
        spread_kernel,
        in_specs=[VMEM] * len(pieces),
        out_specs=VMEM,
        out_shape=jax.ShapeDtypeStruct((rows, cols * len(pieces)), F32),
        compiler_params=params(16),
        name="spread",
    )(*pieces)


def swap(x, group, shard):
    n = lax.axis_size("shard")
    flip = group * n + shard
    pairs = [(i, i ^ flip) for i in range(lax.axis_size("group") * n)]
    return lax.ppermute(x, ("group", "shard"), pairs)


def odd(k):
    return bin(k).count("1") % 2


def reverse(k, count):
    bits = count.bit_length() - 1
    return sum(((k >> i) & 1) << (bits - 1 - i) for i in range(bits))


def chip(k):
    return 2 * k + odd(k)


def local(tokens, w_qk, w_in, w_out, particles, cotangent, clusters, owners):
    n_group, n_shard = lax.axis_size("group"), lax.axis_size("shard")
    parts = math.gcd(n_group, 4)
    pairs = n_shard // 2
    t_rows = tokens.shape[0]
    channels = particles.shape[1]
    cols = w_qk.shape[1] // parts
    part = lax.rem(lax.axis_index("group"), parts)

    w_own = lax.dynamic_slice_in_dim(w_qk, part * cols, cols, axis=1)
    bits = [pairs >> i for i in range(1, pairs.bit_length())]
    first = [w_own[None]]
    for k in bits[:-1]:
        first.append(swap(jnp.concatenate(first), 0, chip(k)))
    tok_x = swap(tokens[None], 1, 1)
    tok = jnp.concatenate([tokens[None], tok_x])
    for k in [1 << i for i in range(1, parts.bit_length() - 1)]:
        tok = jnp.concatenate([tok, swap(tok, k, 1)])

    keep, give = pool(particles, cotangent, clusters, owners, t_rows, n_shard)
    got = swap(give, 0, 1)
    got, first[-1], tok_x = lax.optimization_barrier((got, first[-1], tok_x))
    first = jnp.concatenate(first)
    joined = keep + got.astype(F32)
    got = [swap(joined[k].astype(BF16), 0, chip(k)) for k in [2, 1, *range(3, pairs)]]
    far_first = swap(first, 0, 1)
    second = swap(first, 0, chip(1))
    sums = joined[0]
    for piece in got:
        sums = sums + piece.astype(F32)
    counts = jnp.sum(sums[:, 2 * channels :], axis=1, keepdims=True)
    pooled = jnp.concatenate(
        [sums[:, :channels] / jnp.maximum(counts, 1.0), sums[:, channels : 2 * channels]], axis=1
    ).astype(BF16)
    pooled = [pooled] + [swap(pooled, k, odd(k)) for k in range(1, parts)]
    second, pooled = lax.optimization_barrier((second, pooled))
    far_second = swap(second, 0, 1)
    tok = [tokens, tok_x[0]] + [tok[k] for k in range(2, parts)]
    hid, query = hidden(tok, pooled, first, far_first, w_in)
    up, keep, give = attend(pooled, hid, query, second, far_second, w_out)
    joined = keep.astype(F32) + swap(give, 0, 1).astype(F32)

    unpooled = up[0].astype(F32)
    for k in [*range(2, parts), 1]:
        unpooled = unpooled + swap(up[k], k, odd(k)).astype(F32)
    near = unpooled.astype(BF16)[None]
    for k in [1 << i for i in range(pairs.bit_length() - 1)]:
        near = jnp.concatenate([near, swap(near, 0, chip(k))])
    far = swap(near, 0, 1)
    particle_out = unpool(particles, clusters, owners, near, far)

    grad = joined[0]
    for k in [pairs - 1, *range(pairs - 2, 0, -1)]:
        grad = grad + swap(joined[k].astype(BF16), 0, chip(k)).astype(F32)
    grad = grad.astype(BF16)
    if n_group > parts:
        part_sum = grad
        grad = grad.astype(F32)
        for k in range(1, n_group // parts):
            grad = grad + swap(part_sum, k * parts, 0).astype(F32)
        grad = grad.astype(BF16)
    pieces = {k: swap(grad, k, 1) for k in [*range(1, parts), 0]}
    qk_grad = spread([pieces[k] for k in range(parts)])
    return (particle_out, qk_grad)


def solution(mesh):
    placed = (
        P(("group", "shard"), None),
        P("shard", None),
        P(),
        P(),
        P(("group", "shard"), None),
        P(("group", "shard"), None),
        P(("group", "shard")),
        P(("group", "shard")),
    )
    return jax.shard_map(
        local,
        mesh=mesh,
        in_specs=placed,
        out_specs=(P(("group", "shard"), None), P("shard", None)),
        check_vma=False,
    )
```
